256 devices in a mesh: sta: 64 (over y, z, core), grp: 4 (over x).
Axes of the slice: x: 4, y: 4, z: 8, core: 2. Of those that a mesh axis runs over, the one named last changes fastest.
Arguments:
- records: bfloat16 [4096, 4096], P('grp', 'sta'), may hold values from -150 to 150
- pair_list: int32 [2048, 128, 2], P(('sta', 'grp')), may hold values from 0 to 4095, as said below
- live_blocks: int32 [256], P(('sta', 'grp')), may hold values from 1 to 8, as said below
Outputs:
- correlations: float32 [2048, 128, 1024], P(('sta', 'grp'))
The draws below stay inside these ranges and needn't reach their ends.
Inputs may be any that keep to these rules, and one draw needn't show every extreme that they name: `pair_list`: each pair names two different stations. Writing a station as n * 1024 + c * 16 + k with 0 <= k < 16 (network n, column c), every pair of block b has its first station in column b // 32 and its second station in the same column or at most 2 columns higher. `live_blocks`: some device has all 8 slots in use; the slots in use on a device come first.
All inputs are finite; a program needn't handle non-finite values.
Results may differ from the reference program's by a relative error of at most 0.0073.
Values may be sent and summed in bfloat16 or wider, within the bound.
No kernel may reach another device: no remote copies, remote signals or barrier semaphores. Data moves between devices by JAX's collectives and lax.ppermute only.
A program may use at most 64 MiB of HBM per device.

```python
import math
import jax
import jax.numpy as jnp
from jax import lax

STA_DEV = 16
WINDOW_COUNT = 4
WINDOW_POINTS = 1024
HALF = 16
BLOCK = 128
REACH = 2
BLK_CAP = 8
NF = 512
TIME = 4096
COLS = 64
NETS = 4
QUARTER = 1024
SENSOR_COUNT = 4096
NBLK = 2048
DEVICES = 256


def draw_records(key, part):
    key = jax.random.fold_in(key, 5)
    stochastic_seeds = jax.random.split(key, 4)
    samples_raw = jnp.clip(jax.random.normal(stochastic_seeds[0], (SENSOR_COUNT, TIME + 1), jnp.float32), -5.0, 5.0)
    upper_level = 5.0
    colour = jax.random.uniform(stochastic_seeds[1], (SENSOR_COUNT, 1), jnp.float32, -0.85, 0.85)
    disturbance_amplitudes = jnp.exp(jax.random.uniform(stochastic_seeds[2], (SENSOR_COUNT, 1, 1), jnp.float32, math.log(0.5), math.log(upper_level)))
    impulse_disturbance = jnp.exp(jax.random.uniform(stochastic_seeds[3], (SENSOR_COUNT, WINDOW_COUNT, 1), jnp.float32, 0.0, math.log(3.0)))
    tinted_disturbance = (samples_raw[:, 1:] + colour * samples_raw[:, :-1]) * jax.lax.rsqrt(1.0 + colour * colour)
    filtered_disturbance = tinted_disturbance.reshape(SENSOR_COUNT, WINDOW_COUNT, WINDOW_POINTS) * disturbance_amplitudes * impulse_disturbance
    return filtered_disturbance.reshape(SENSOR_COUNT, TIME).astype(jnp.bfloat16)


def draw_pair_list(key, part):
    key = jax.random.fold_in(key, 11)
    stochastic_seeds = jax.random.split(key, 5)
    shape = (NBLK, BLOCK)
    column = (jnp.arange(NBLK, dtype=jnp.int32) // (BLK_CAP * NETS))[:, None]
    first_net = jax.random.randint(stochastic_seeds[0], shape, 0, NETS)
    first_pos = jax.random.randint(stochastic_seeds[1], shape, 0, STA_DEV)
    offset = jax.random.randint(stochastic_seeds[2], shape, 0, REACH + 1)
    second_col = jnp.minimum(column + offset, COLS - 1)
    second_net = jax.random.randint(stochastic_seeds[3], shape, 0, NETS)
    second_pos = (first_pos + jax.random.randint(stochastic_seeds[4], shape, 1, STA_DEV)) % STA_DEV
    first_station = first_net * QUARTER + column * STA_DEV + first_pos
    second_station = second_net * QUARTER + second_col * STA_DEV + second_pos
    return jnp.stack([first_station, second_station], axis=-1).astype(jnp.int32)


def draw_live_blocks(key, part):
    key = jax.random.fold_in(key, 23)
    stochastic_seeds = jax.random.split(key, 3)
    first_count = jax.random.randint(stochastic_seeds[0], (DEVICES,), 1, BLK_CAP + 1)
    second_count = jax.random.randint(stochastic_seeds[1], (DEVICES,), 1, BLK_CAP + 1)
    counts_live = jnp.minimum(first_count, second_count)
    busiest = jax.random.randint(stochastic_seeds[2], (), 0, DEVICES)
    return counts_live.at[busiest].set(BLK_CAP).astype(jnp.int32)


def setup_inputs(seed: int = 0) -> dict:
    arg_keys = jax.random.split(jax.random.key(seed), 4)
    return {
        "records": draw_records(jax.random.fold_in(arg_keys[3], 71), 0),
        "pair_list": draw_pair_list(jax.random.fold_in(arg_keys[3], 71), 0),
        "live_blocks": draw_live_blocks(jax.random.fold_in(arg_keys[3], 71), 0),
    }


def forward_table(trace_duration, bin_count):
    impulse_moments = jnp.arange(trace_duration, dtype=jnp.int32)[:, None]
    spectral_position = jnp.arange(1, bin_count + 1, dtype=jnp.int32)[None, :]
    spectral_rotations = (impulse_moments * spectral_position % trace_duration).astype(jnp.float32) * (2.0 * math.pi / trace_duration)
    factor = 1.0 / math.sqrt(trace_duration)
    return (jnp.concatenate([jnp.cos(spectral_rotations), -jnp.sin(spectral_rotations)], axis=1) * factor).astype(jnp.bfloat16)

def lag_table(trace_duration, bin_count, segment_count):
    spectral_position = jnp.arange(1, bin_count + 1, dtype=jnp.int32)[:, None]
    lag_index = jnp.arange(trace_duration, dtype=jnp.int32)[None, :] - trace_duration // 2
    spectral_rotations = (spectral_position * lag_index % trace_duration).astype(jnp.float32) * (2.0 * math.pi / trace_duration)
    factor = 1.0 / math.sqrt(bin_count * segment_count)
    return (jnp.concatenate([jnp.cos(spectral_rotations), -jnp.sin(spectral_rotations)], axis=0) * factor).astype(jnp.bfloat16)

def smoother(bin_count, half_width, segment_count):
    positions = jnp.arange(bin_count, dtype=jnp.int32)
    inside = (jnp.abs(positions[:, None] - positions[None, :]) <= half_width).astype(jnp.float32)
    totals = lax.optimization_barrier(jnp.sum(inside, axis=0))
    return inside / (totals * segment_count)[None, :]

def whiten(segments, forward, weights):
    stations, segment_count, trace_duration = segments.shape
    bin_count = weights.shape[0]
    spectra = jnp.dot(segments.reshape(stations * segment_count, trace_duration), forward, preferred_element_type=jnp.float32)
    spectra = spectra.reshape(stations, segment_count, 2 * bin_count)
    energy = lax.optimization_barrier(jnp.sum(spectra * spectra, axis=1))
    energy = energy[:, :bin_count] + energy[:, bin_count:]
    disturbance_amplitudes = jnp.dot(energy, weights, precision=lax.Precision.HIGHEST)
    scaling = lax.rsqrt(disturbance_amplitudes + 1e-06)
    scaling = jnp.concatenate([scaling, scaling], axis=1)
    return (spectra * scaling[:, None, :]).astype(jnp.bfloat16)

def cross_spectra(first_rows, second_rows):
    bin_count = first_rows.shape[2] // 2
    first_re = first_rows[:, :, :bin_count].astype(jnp.float32)
    first_im = first_rows[:, :, bin_count:].astype(jnp.float32)
    second_re = second_rows[:, :, :bin_count].astype(jnp.float32)
    second_im = second_rows[:, :, bin_count:].astype(jnp.float32)
    real_part = lax.optimization_barrier(jnp.sum(first_re * second_re + first_im * second_im, axis=1))
    imag_part = lax.optimization_barrier(jnp.sum(first_im * second_re - first_re * second_im, axis=1))
    return jnp.concatenate([real_part, imag_part], axis=1).astype(jnp.bfloat16)

def reference(records, pair_list, live_blocks):
    forward = forward_table(WINDOW_POINTS, NF)
    weights = smoother(NF, HALF, WINDOW_COUNT)
    whitened = whiten(records.reshape(SENSOR_COUNT, WINDOW_COUNT, WINDOW_POINTS), forward, weights)
    inverse = lag_table(WINDOW_POINTS, NF, WINDOW_COUNT)
    slot_index = jnp.arange(NBLK, dtype=jnp.int32) % BLK_CAP
    owners = jnp.arange(NBLK, dtype=jnp.int32) // BLK_CAP
    keep_mask = (slot_index < live_blocks[owners]).astype(jnp.float32)

    def one_block(block_rows):
        pairs_now, keep_now = block_rows
        mixed_spectra = cross_spectra(whitened[pairs_now[:, 0]], whitened[pairs_now[:, 1]])
        return jnp.dot(mixed_spectra, inverse, preferred_element_type=jnp.float32) * keep_now
    return lax.map(one_block, (pair_list, keep_mask))
```

```python
import math

import jax
import jax.numpy as jnp
import ml_dtypes
import numpy as np
from jax import lax
from jax.experimental import pallas as pl
from jax.experimental.pallas import tpu as pltpu
from jax.sharding import PartitionSpec as P

SEGMENTS = 4
POINTS = 1024
BINS = 512
HALF = 16
BLOCK = 128
NETS = 4
PER = 16
SLOTS = 3
ROWS = 32
LANES = 128
STEP_PAIRS = 256

BIN_ORDER = np.concatenate([np.arange(2, BINS + 1, 2), np.arange(1, BINS + 1, 2)])


def forward_table():
    t = np.arange(POINTS, dtype=np.int64)[:, None]
    turn = (t * BIN_ORDER[None, :] % POINTS) * (2.0 * math.pi / POINTS)
    table = np.concatenate([np.cos(turn), -np.sin(turn)], axis=1) / math.sqrt(POINTS)
    return table.astype(np.float32).astype(ml_dtypes.bfloat16)


def lag_tables():
    lag = np.arange(POINTS // 2, dtype=np.int64)[None, :] - POINTS // 2
    tables = []
    for bins in (BIN_ORDER[: BINS // 2], BIN_ORDER[BINS // 2 :]):
        turn = (bins[:, None] * lag % POINTS) * (2.0 * math.pi / POINTS)
        table = np.concatenate([np.cos(turn), -np.sin(turn)], axis=0) / math.sqrt(BINS * SEGMENTS)
        tables.append(table.astype(np.float32).astype(ml_dtypes.bfloat16))
    return tables


def band_tables():
    near = np.abs(BIN_ORDER[:, None] - BIN_ORDER[None, :]) <= HALF
    share = 1.0 / (near.sum(axis=0) * SEGMENTS)
    return near.astype(np.float32).astype(ml_dtypes.bfloat16), share.astype(np.float32)[None, :]


def pack_kernel(records_ref, out_ref):
    samples, stations = records_ref.shape
    own = records_ref[...].astype(jnp.float32)
    ahead = jnp.concatenate([own[:, 2 * PER :], own[:, : 2 * PER]], axis=1)
    both = jnp.concatenate([own, ahead], axis=0)
    for block in range(stations // LANES):
        part = both[:, block * LANES : (block + 1) * LANES]
        out_ref[block * LANES : (block + 1) * LANES, :] = part.T.astype(jnp.bfloat16)


def whiten_kernel(parts_ref, forward_ref, band_ref, share_ref, both_ref, given_ref, segs, wide):
    core = lax.rem(lax.axis_index("sta"), 2)
    low = lax.broadcasted_iota(jnp.int32, (PER, LANES), 1) < LANES // 2
    for e in range(SEGMENTS):
        for u in range(POINTS // LANES):
            row = (e * POINTS // LANES + u) * 2 * PER
            first = parts_ref[row : row + PER, :].astype(jnp.float32)
            second = parts_ref[row + PER : row + 2 * PER, :].astype(jnp.float32)
            near = jnp.where(low, first, pltpu.roll(second, LANES // 2, 1))
            far = jnp.where(low, pltpu.roll(first, LANES // 2, 1), second)
            segs[e * PER : (e + 1) * PER, u * LANES : (u + 1) * LANES] = near.astype(jnp.bfloat16)
            segs[(SEGMENTS + e) * PER : (SEGMENTS + e + 1) * PER, u * LANES : (u + 1) * LANES] = (
                far.astype(jnp.bfloat16)
            )
    spectra = jnp.dot(segs[...], forward_ref[...], preferred_element_type=jnp.float32)
    squares = (spectra * spectra).reshape(2, SEGMENTS, PER, 2 * BINS)
    energy = jnp.sum(squares, axis=1).reshape(2 * PER, 2 * BINS)
    energy = energy[:, :BINS] + energy[:, BINS:]
    top = energy.astype(jnp.bfloat16)
    rest = energy - top.astype(jnp.float32)
    middle = rest.astype(jnp.bfloat16)
    bottom = (rest - middle.astype(jnp.float32)).astype(jnp.bfloat16)
    split = jnp.concatenate([top, middle, bottom], axis=0)
    sums = jnp.dot(split, band_ref[...], preferred_element_type=jnp.float32)
    count = 2 * PER
    total = sums[:count] + (sums[count : 2 * count] + sums[2 * count :])
    scale = lax.rsqrt(total * share_ref[...] + 1e-06)
    for column in range(2):
        for e in range(SEGMENTS):
            for k in range(0, PER, 8):
                for part in range(2):
                    for j in range(BINS // LANES):
                        at = (column * SEGMENTS + e) * PER + k
                        lane = part * BINS + j * LANES
                        piece = (
                            spectra[at : at + 8, lane : lane + LANES]
                            * scale[column * PER + k : column * PER + k + 8, j * LANES : (j + 1) * LANES]
                        )
                        row = (column * PER + k) * ROWS + part * (ROWS // 2) + e * (BINS // LANES) + j
                        wide[pl.ds(row, 8, stride=ROWS), :] = piece
    size = PER * ROWS
    given = 1 - core
    given_rows = wide[pl.ds(pl.multiple_of(given * size, size), size), :].astype(jnp.bfloat16)
    other_rows = wide[pl.ds(pl.multiple_of(core * size, size), size), :].astype(jnp.bfloat16)
    both_ref[:size, :] = given_rows
    both_ref[size:, :] = other_rows
    given_ref[...] = given_rows


def pair_kernel(
    live_ref, index_ref, even_ref, odd_ref, p0, p1, p2, p3, s0, s1, s2, s3, out_ref, table, mixed
):
    step = pl.program_id(0)
    size = PER * ROWS
    half = ROWS // 4

    @pl.when(step == 0)
    def _():
        for net, (pieces, swapped) in enumerate(((p0, s0), (p1, s1), (p2, s2), (p3, s3))):
            for slot in range(SLOTS):
                source = swapped if slot == 2 else pieces
                start = 0 if slot == 2 else slot * size
                for k in range(PER):
                    table[(slot * NETS + net) * PER + k] = source[
                        start + k * ROWS : start + (k + 1) * ROWS, :
                    ].astype(jnp.float32)

    upper = lax.broadcasted_iota(jnp.int32, (8, LANES), 0) < 4

    def mix(q):
        packed = index_ref[step * STEP_PAIRS + q]
        i = packed & 255
        j = packed >> 8
        ar0, ar1 = table[i, 0:half], table[i, half : 2 * half]
        ai0, ai1 = table[i, 2 * half : 3 * half], table[i, 3 * half : 4 * half]
        br0, br1 = table[j, 0:half], table[j, half : 2 * half]
        bi0, bi1 = table[j, 2 * half : 3 * half], table[j, 3 * half : 4 * half]
        real = (ar0 * br0 + ar1 * br1) + (ai0 * bi0 + ai1 * bi1)
        imag = (ai0 * br0 + ai1 * br1) - (ar0 * bi0 + ar1 * bi1)
        turned = pltpu.roll(jnp.where(upper, imag, real), 4, 0)
        mixed[pl.ds(pl.multiple_of(q * 8, 8), 8), :] = jnp.where(upper, real, imag) + turned

    def some(g, carry):
        for q in range(8):
            mix(g * 8 + q)
        return carry

    lax.fori_loop(0, STEP_PAIRS // 8, some, 0)

    def rows_of(blocks):
        return jnp.concatenate(
            [mixed[pl.ds(b, STEP_PAIRS, stride=8), :].astype(jnp.bfloat16) for b in blocks], axis=1
        )

    even = jnp.dot(rows_of((0, 1, 4, 5)), even_ref[...], preferred_element_type=jnp.float32)
    odd = jnp.dot(rows_of((2, 3, 6, 7)), odd_ref[...], preferred_element_type=jnp.float32)
    for b in range(STEP_PAIRS // BLOCK):
        keep = (step * (STEP_PAIRS // BLOCK) + b < live_ref[0]).astype(jnp.float32)
        here = slice(b * BLOCK, (b + 1) * BLOCK)
        out_ref[here, : POINTS // 2] = (even[here] + odd[here]) * keep
        out_ref[here, POINTS // 2 :] = (even[here] - odd[here]) * keep


def local(records, pair_list, live_blocks):
    columns = lax.axis_size("sta")
    nets = lax.axis_size("grp")
    column = lax.axis_index("sta")
    net = lax.axis_index("grp")
    core = column % 2
    vmem = pl.BlockSpec(memory_space=pltpu.VMEM)
    smem = pl.BlockSpec(memory_space=pltpu.SMEM)
    messages = pl.pallas_call(
        pack_kernel,
        out_shape=jax.ShapeDtypeStruct((columns * PER, LANES), jnp.bfloat16),
        in_specs=[vmem],
        out_specs=vmem,
    )(records.T)
    received = lax.all_to_all(
        messages.reshape(columns, PER, LANES), "sta", split_axis=0, concat_axis=0, tiled=True
    ).reshape(columns * PER, LANES)
    band, share = band_tables()
    size = PER * ROWS
    both, given = pl.pallas_call(
        whiten_kernel,
        out_shape=(
            jax.ShapeDtypeStruct((2 * size, LANES), jnp.bfloat16),
            jax.ShapeDtypeStruct((size, LANES), jnp.bfloat16),
        ),
        in_specs=[vmem] * 4,
        out_specs=(vmem, vmem),
        scratch_shapes=[
            pltpu.VMEM((2 * SEGMENTS * PER, POINTS), jnp.bfloat16),
            pltpu.VMEM((2 * size, LANES), jnp.float32),
        ],
    )(received, jnp.asarray(forward_table()), jnp.asarray(band), jnp.asarray(share))
    swap = [(i, i ^ 1) for i in range(columns)]
    pieces, swapped = [both], [lax.ppermute(given, "sta", swap)]
    for by in range(1, nets):
        piece = lax.ppermute(both, "grp", [((i + by) % nets, i) for i in range(nets)])
        pieces.append(piece)
        swapped.append(lax.ppermute(piece[:size], "sta", swap))

    station_net = pair_list // (columns * PER)
    offset = pair_list // PER % columns - column
    slot = jnp.where(offset == 1, 2, jnp.where(offset == 0, 1 - core, core))
    place = (slot * nets + (station_net - net) % nets) * PER + pair_list % PER
    index = (place[:, :, 0] + 256 * place[:, :, 1]).reshape(-1)
    even, odd = lag_tables()
    pairs = index.shape[0]
    return pl.pallas_call(
        pair_kernel,
        grid=(pairs // STEP_PAIRS,),
        out_shape=jax.ShapeDtypeStruct((pairs, POINTS), jnp.float32),
        in_specs=[smem, smem] + [vmem] * 10,
        out_specs=pl.BlockSpec((STEP_PAIRS, POINTS), lambda i: (i, 0)),
        scratch_shapes=[
            pltpu.VMEM((SLOTS * NETS * PER, ROWS, LANES), jnp.float32),
            pltpu.VMEM((STEP_PAIRS * 8, LANES), jnp.float32),
        ],
        compiler_params=pltpu.CompilerParams(vmem_limit_bytes=40 * 2**20),
    )(live_blocks, index, jnp.asarray(even), jnp.asarray(odd), *pieces, *swapped).reshape(
        pair_list.shape[0], BLOCK, POINTS
    )


def solution(mesh):
    in_specs = (P("grp", "sta"), P(("sta", "grp"), None, None), P(("sta", "grp")))
    out_specs = P(("sta", "grp"), None, None)
    return jax.shard_map(local, mesh=mesh, in_specs=in_specs, out_specs=out_specs, check_vma=False)
```

```python
import math

import jax
import jax.numpy as jnp
import ml_dtypes
import numpy as np
from jax import lax
from jax.experimental import pallas as pl
from jax.experimental.pallas import tpu as pltpu
from jax.sharding import PartitionSpec as P

SEGMENTS = 4
POINTS = 1024
BINS = 512
HALF = 16
BLOCK = 128
NETS = 4
PER = 16
SLOTS = 3
ROWS = 32
LANES = 128
STEP_PAIRS = 256

BIN_ORDER = np.concatenate([np.arange(2, BINS + 1, 2), np.arange(1, BINS + 1, 2)])


def forward_table():
    t = np.arange(POINTS, dtype=np.int64)[:, None]
    turn = (t * BIN_ORDER[None, :] % POINTS) * (2.0 * math.pi / POINTS)
    table = np.concatenate([np.cos(turn), -np.sin(turn)], axis=1) / math.sqrt(POINTS)
    return table.astype(np.float32).astype(ml_dtypes.bfloat16)


def lag_tables():
    lag = np.arange(POINTS // 2, dtype=np.int64)[None, :] - POINTS // 2
    tables = []
    for bins in (BIN_ORDER[: BINS // 2], BIN_ORDER[BINS // 2 :]):
        turn = (bins[:, None] * lag % POINTS) * (2.0 * math.pi / POINTS)
        table = np.concatenate([np.cos(turn), -np.sin(turn)], axis=0) / math.sqrt(BINS * SEGMENTS)
        tables.append(table.astype(np.float32).astype(ml_dtypes.bfloat16))
    return tables


def band_tables():
    near = np.abs(BIN_ORDER[:, None] - BIN_ORDER[None, :]) <= HALF
    share = 1.0 / (near.sum(axis=0) * SEGMENTS)
    return near.astype(np.float32).astype(ml_dtypes.bfloat16), share.astype(np.float32)[None, :]


def pack_kernel(records_ref, out_ref):
    samples, stations = records_ref.shape
    own = records_ref[...].astype(jnp.float32)
    ahead = jnp.concatenate([own[:, 2 * PER :], own[:, : 2 * PER]], axis=1)
    both = jnp.concatenate([own, ahead], axis=0)
    for block in range(stations // LANES):
        part = both[:, block * LANES : (block + 1) * LANES]
        out_ref[block * LANES : (block + 1) * LANES, :] = part.T.astype(jnp.bfloat16)


def whiten_kernel(
    parts_ref, forward_ref, band_ref, share_ref, both_ref, given_ref, other_ref, segs, wide
):
    core = lax.rem(lax.axis_index("sta"), 2)
    low = lax.broadcasted_iota(jnp.int32, (PER, LANES), 1) < LANES // 2
    for e in range(SEGMENTS):
        for u in range(POINTS // LANES):
            row = (e * POINTS // LANES + u) * 2 * PER
            first = parts_ref[row : row + PER, :].astype(jnp.float32)
            second = parts_ref[row + PER : row + 2 * PER, :].astype(jnp.float32)
            near = jnp.where(low, first, pltpu.roll(second, LANES // 2, 1))
            far = jnp.where(low, pltpu.roll(first, LANES // 2, 1), second)
            segs[e * PER : (e + 1) * PER, u * LANES : (u + 1) * LANES] = near.astype(jnp.bfloat16)
            segs[(SEGMENTS + e) * PER : (SEGMENTS + e + 1) * PER, u * LANES : (u + 1) * LANES] = (
                far.astype(jnp.bfloat16)
            )
    spectra = jnp.dot(segs[...], forward_ref[...], preferred_element_type=jnp.float32)
    squares = (spectra * spectra).reshape(2, SEGMENTS, PER, 2 * BINS)
    energy = jnp.sum(squares, axis=1).reshape(2 * PER, 2 * BINS)
    energy = energy[:, :BINS] + energy[:, BINS:]
    top = energy.astype(jnp.bfloat16)
    rest = energy - top.astype(jnp.float32)
    middle = rest.astype(jnp.bfloat16)
    bottom = (rest - middle.astype(jnp.float32)).astype(jnp.bfloat16)
    split = jnp.concatenate([top, middle, bottom], axis=0)
    sums = jnp.dot(split, band_ref[...], preferred_element_type=jnp.float32)
    count = 2 * PER
    total = sums[:count] + (sums[count : 2 * count] + sums[2 * count :])
    scale = lax.rsqrt(total * share_ref[...] + 1e-06)
    for column in range(2):
        for e in range(SEGMENTS):
            for k in range(0, PER, 8):
                for part in range(2):
                    for j in range(BINS // LANES):
                        at = (column * SEGMENTS + e) * PER + k
                        lane = part * BINS + j * LANES
                        piece = (
                            spectra[at : at + 8, lane : lane + LANES]
                            * scale[column * PER + k : column * PER + k + 8, j * LANES : (j + 1) * LANES]
                        )
                        row = (column * PER + k) * ROWS + part * (ROWS // 2) + e * (BINS // LANES) + j
                        wide[pl.ds(row, 8, stride=ROWS), :] = piece
    size = PER * ROWS
    given = 1 - core
    given_rows = wide[pl.ds(pl.multiple_of(given * size, size), size), :].astype(jnp.bfloat16)
    other_rows = wide[pl.ds(pl.multiple_of(core * size, size), size), :].astype(jnp.bfloat16)
    both_ref[:size, :] = given_rows
    both_ref[size:, :] = other_rows
    given_ref[...] = given_rows
    other_ref[...] = other_rows


def pair_kernel(
    live_ref, index_ref, even_ref, odd_ref, b0, b1, g2, o2, b3, s0, s1, s2, s3, out_ref, table, mixed
):
    step = pl.program_id(0)
    size = PER * ROWS
    half = ROWS // 4

    @pl.when(step == 0)
    def _():
        sources = (
            ((b0, 0), (b0, size), (s0, 0)),
            ((b1, 0), (b1, size), (s1, 0)),
            ((g2, 0), (o2, 0), (s2, 0)),
            ((b3, 0), (b3, size), (s3, 0)),
        )
        for net in range(NETS):
            for slot in range(SLOTS):
                source, start = sources[net][slot]
                for k in range(PER):
                    at = start + k * ROWS
                    table[(slot * NETS + net) * PER + k] = source[at : at + ROWS, :].astype(
                        jnp.float32
                    )

    upper = lax.broadcasted_iota(jnp.int32, (8, LANES), 0) < 4

    def mix(q):
        packed = index_ref[step * STEP_PAIRS + q]
        i = packed & 255
        j = packed >> 8
        ar0, ar1 = table[i, 0:half], table[i, half : 2 * half]
        ai0, ai1 = table[i, 2 * half : 3 * half], table[i, 3 * half : 4 * half]
        br0, br1 = table[j, 0:half], table[j, half : 2 * half]
        bi0, bi1 = table[j, 2 * half : 3 * half], table[j, 3 * half : 4 * half]
        real = (ar0 * br0 + ar1 * br1) + (ai0 * bi0 + ai1 * bi1)
        imag = (ai0 * br0 + ai1 * br1) - (ar0 * bi0 + ar1 * bi1)
        turned = pltpu.roll(jnp.where(upper, imag, real), 4, 0)
        mixed[pl.ds(pl.multiple_of(q * 8, 8), 8), :] = jnp.where(upper, real, imag) + turned

    def some(g, carry):
        for q in range(32):
            mix(g * 32 + q)
        return carry

    lax.fori_loop(0, STEP_PAIRS // 32, some, 0)

    def rows_of(blocks):
        return jnp.concatenate(
            [mixed[pl.ds(b, STEP_PAIRS, stride=8), :].astype(jnp.bfloat16) for b in blocks], axis=1
        )

    even = jnp.dot(rows_of((0, 1, 4, 5)), even_ref[...], preferred_element_type=jnp.float32)
    odd = jnp.dot(rows_of((2, 3, 6, 7)), odd_ref[...], preferred_element_type=jnp.float32)
    for b in range(STEP_PAIRS // BLOCK):
        keep = (step * (STEP_PAIRS // BLOCK) + b < live_ref[0]).astype(jnp.float32)
        here = slice(b * BLOCK, (b + 1) * BLOCK)
        out_ref[here, : POINTS // 2] = (even[here] + odd[here]) * keep
        out_ref[here, POINTS // 2 :] = (even[here] - odd[here]) * keep


def local(records, pair_list, live_blocks):
    columns = lax.axis_size("sta")
    nets = lax.axis_size("grp")
    column = lax.axis_index("sta")
    net = lax.axis_index("grp")
    core = column % 2
    vmem = pl.BlockSpec(memory_space=pltpu.VMEM)
    smem = pl.BlockSpec(memory_space=pltpu.SMEM)
    messages = pl.pallas_call(
        pack_kernel,
        out_shape=jax.ShapeDtypeStruct((columns * PER, LANES), jnp.bfloat16),
        in_specs=[vmem],
        out_specs=vmem,
        compiler_params=pltpu.CompilerParams(vmem_limit_bytes=8 * 2**20),
        cost_estimate=pl.CostEstimate(flops=2 * 10**10, bytes_accessed=3 * 2**17, transcendentals=0),
    )(records.T)
    received = lax.all_to_all(
        messages.reshape(columns, PER, LANES), "sta", split_axis=0, concat_axis=0, tiled=True
    ).reshape(columns * PER, LANES)
    band, share = band_tables()
    size = PER * ROWS
    both, given, other = pl.pallas_call(
        whiten_kernel,
        out_shape=(
            jax.ShapeDtypeStruct((2 * size, LANES), jnp.bfloat16),
            jax.ShapeDtypeStruct((size, LANES), jnp.bfloat16),
            jax.ShapeDtypeStruct((size, LANES), jnp.bfloat16),
        ),
        in_specs=[vmem] * 4,
        out_specs=(vmem, vmem, vmem),
        scratch_shapes=[
            pltpu.VMEM((2 * SEGMENTS * PER, POINTS), jnp.bfloat16),
            pltpu.VMEM((2 * size, LANES), jnp.float32),
        ],
        compiler_params=pltpu.CompilerParams(vmem_limit_bytes=16 * 2**20),
        cost_estimate=pl.CostEstimate(flops=2 * 10**9, bytes_accessed=3 * 2**20, transcendentals=0),
    )(received, jnp.asarray(forward_table()), jnp.asarray(band), jnp.asarray(share))
    def from_net(value, by):
        return lax.ppermute(value, "grp", [((i + by) % nets, i) for i in range(nets)])

    def from_other_core(value):
        return lax.ppermute(value, "sta", [(i, i ^ 1) for i in range(columns)])

    other2, given2 = from_net(other, 2), from_net(given, 2)
    both1, both3 = from_net(both, 1), from_net(both, 3)
    pieces = [both, both1, given2, other2, both3]
    swapped = [from_other_core(part) for part in (given, both1[:size], given2, both3[:size])]

    station_net = pair_list // (columns * PER)
    offset = pair_list // PER % columns - column
    slot = jnp.where(offset == 1, 2, jnp.where(offset == 0, 1 - core, core))
    place = (slot * nets + (station_net - net) % nets) * PER + pair_list % PER
    index = (place[:, :, 0] + 256 * place[:, :, 1]).reshape(-1)
    even, odd = lag_tables()
    pairs = index.shape[0]
    return pl.pallas_call(
        pair_kernel,
        grid=(pairs // STEP_PAIRS,),
        out_shape=jax.ShapeDtypeStruct((pairs, POINTS), jnp.float32),
        in_specs=[smem, smem] + [vmem] * 11,
        out_specs=pl.BlockSpec((STEP_PAIRS, POINTS), lambda i: (i, 0)),
        scratch_shapes=[
            pltpu.VMEM((SLOTS * NETS * PER, ROWS, LANES), jnp.float32),
            pltpu.VMEM((STEP_PAIRS * 8, LANES), jnp.float32),
        ],
        compiler_params=pltpu.CompilerParams(vmem_limit_bytes=24 * 2**20),
        cost_estimate=pl.CostEstimate(flops=6 * 10**9, bytes_accessed=6 * 2**20, transcendentals=0),
    )(live_blocks, index, jnp.asarray(even), jnp.asarray(odd), *pieces, *swapped).reshape(
        pair_list.shape[0], BLOCK, POINTS
    )


def solution(mesh):
    in_specs = (P("grp", "sta"), P(("sta", "grp"), None, None), P(("sta", "grp")))
    out_specs = P(("sta", "grp"), None, None)
    return jax.shard_map(local, mesh=mesh, in_specs=in_specs, out_specs=out_specs, check_vma=False)
```

```python
import math

import jax
import jax.numpy as jnp
import ml_dtypes
import numpy as np
from jax import lax
from jax.experimental import pallas as pl
from jax.experimental.pallas import tpu as pltpu
from jax.sharding import PartitionSpec as P

SEGMENTS = 4
POINTS = 1024
BINS = 512
HALF = 16
BLOCK = 128
NETS = 4
PER = 16
SLOTS = 3
ROWS = 32
LANES = 128
STEP_PAIRS = 256
UNROLL = 64
ZERO_ROW = SLOTS * NETS * PER * ROWS

BIN_ORDER = np.concatenate([np.arange(2, BINS + 1, 2), np.arange(1, BINS + 1, 2)])


def forward_table():
    t = np.arange(POINTS, dtype=np.int64)[:, None]
    turn = (t * BIN_ORDER[None, :] % POINTS) * (2.0 * math.pi / POINTS)
    table = np.concatenate([np.cos(turn), -np.sin(turn)], axis=1) / math.sqrt(POINTS)
    return table.astype(np.float32).astype(ml_dtypes.bfloat16)


def lag_tables():
    lag = np.arange(POINTS // 2, dtype=np.int64)[None, :] - POINTS // 2
    tables = []
    for bins in (BIN_ORDER[: BINS // 2], BIN_ORDER[BINS // 2 :]):
        turn = (bins[:, None] * lag % POINTS) * (2.0 * math.pi / POINTS)
        table = np.concatenate([np.cos(turn), -np.sin(turn)], axis=0) / math.sqrt(BINS * SEGMENTS)
        tables.append(table.astype(np.float32).astype(ml_dtypes.bfloat16))
    return tables


def band_tables():
    near = np.abs(BIN_ORDER[:, None] - BIN_ORDER[None, :]) <= HALF
    share = 1.0 / (near.sum(axis=0) * SEGMENTS)
    return near.astype(np.float32).astype(ml_dtypes.bfloat16), share.astype(np.float32)[None, :]


def pack_kernel(records_ref, out_ref):
    samples, stations = records_ref.shape
    own = records_ref[...].astype(jnp.float32)
    ahead = jnp.concatenate([own[:, 2 * PER :], own[:, : 2 * PER]], axis=1)
    both = jnp.concatenate([own, ahead], axis=0)
    for block in range(stations // LANES):
        part = both[:, block * LANES : (block + 1) * LANES]
        out_ref[block * LANES : (block + 1) * LANES, :] = part.T.astype(jnp.bfloat16)


def whiten_kernel(
    parts_ref, forward_ref, band_ref, share_ref, both_ref, given_ref, other_ref, segs, wide
):
    core = lax.rem(lax.axis_index("sta"), 2)
    low = lax.broadcasted_iota(jnp.int32, (PER, LANES), 1) < LANES // 2
    for e in range(SEGMENTS):
        for u in range(POINTS // LANES):
            row = (e * POINTS // LANES + u) * 2 * PER
            first = parts_ref[row : row + PER, :].astype(jnp.float32)
            second = parts_ref[row + PER : row + 2 * PER, :].astype(jnp.float32)
            near = jnp.where(low, first, pltpu.roll(second, LANES // 2, 1))
            far = jnp.where(low, pltpu.roll(first, LANES // 2, 1), second)
            segs[e * PER : (e + 1) * PER, u * LANES : (u + 1) * LANES] = near.astype(jnp.bfloat16)
            segs[(SEGMENTS + e) * PER : (SEGMENTS + e + 1) * PER, u * LANES : (u + 1) * LANES] = (
                far.astype(jnp.bfloat16)
            )
    spectra = jnp.dot(segs[...], forward_ref[...], preferred_element_type=jnp.float32)
    squares = (spectra * spectra).reshape(2, SEGMENTS, PER, 2 * BINS)
    energy = jnp.sum(squares, axis=1).reshape(2 * PER, 2 * BINS)
    energy = energy[:, :BINS] + energy[:, BINS:]
    top = energy.astype(jnp.bfloat16)
    rest = energy - top.astype(jnp.float32)
    middle = rest.astype(jnp.bfloat16)
    bottom = (rest - middle.astype(jnp.float32)).astype(jnp.bfloat16)
    split = jnp.concatenate([top, middle, bottom], axis=0)
    sums = jnp.dot(split, band_ref[...], preferred_element_type=jnp.float32)
    count = 2 * PER
    total = sums[:count] + (sums[count : 2 * count] + sums[2 * count :])
    scale = lax.rsqrt(total * share_ref[...] + 1e-06)
    for column in range(2):
        for e in range(SEGMENTS):
            for k in range(0, PER, 8):
                for part in range(2):
                    for j in range(BINS // LANES):
                        at = (column * SEGMENTS + e) * PER + k
                        lane = part * BINS + j * LANES
                        piece = (
                            spectra[at : at + 8, lane : lane + LANES]
                            * scale[column * PER + k : column * PER + k + 8, j * LANES : (j + 1) * LANES]
                        )
                        row = (column * PER + k) * ROWS + part * (ROWS // 2) + e * (BINS // LANES) + j
                        wide[pl.ds(row, 8, stride=ROWS), :] = piece
    size = PER * ROWS
    given = 1 - core
    given_rows = wide[pl.ds(pl.multiple_of(given * size, size), size), :].astype(jnp.bfloat16)
    other_rows = wide[pl.ds(pl.multiple_of(core * size, size), size), :].astype(jnp.bfloat16)
    both_ref[:size, :] = given_rows
    both_ref[size:, :] = other_rows
    given_ref[...] = given_rows
    other_ref[...] = other_rows


def pair_kernel(
    index_ref, even_ref, odd_ref, b0, b1, g2, o2, b3, s0, s1, s2, s3, out_ref, *scratch
):
    table, reals, imags, result, places, place_sem, sems = scratch
    size = PER * ROWS
    half = ROWS // 4
    pairs = index_ref.shape[0] // 2
    load_places = pltpu.make_async_copy(index_ref, places, place_sem)
    load_places.start()
    sources = (
        ((b0, 0), (b0, size), (s0, 0)),
        ((b1, 0), (b1, size), (s1, 0)),
        ((g2, 0), (o2, 0), (s2, 0)),
        ((b3, 0), (b3, size), (s3, 0)),
    )
    for net in range(NETS):
        for slot in range(SLOTS):
            source, start = sources[net][slot]
            row = (slot * NETS + net) * size
            table[row : row + size, :] = source[start : start + size, :].astype(jnp.float32)
    table[ZERO_ROW : ZERO_ROW + ROWS, :] = jnp.zeros((ROWS, LANES), jnp.float32)
    load_places.wait()

    def mix(step, q):
        at = step * STEP_PAIRS + q
        first = table[pl.ds(pl.multiple_of(places[at], ROWS), ROWS), :]
        second = table[pl.ds(pl.multiple_of(places[pairs + at], ROWS), ROWS), :]
        ar0, ar1, ai0, ai1 = (first[n : n + half] for n in range(0, ROWS, half))
        br0, br1, bi0, bi1 = (second[n : n + half] for n in range(0, ROWS, half))
        rows = pl.ds(pl.multiple_of(q * half, half), half)
        reals[rows, :] = (ar0 * br0 + ar1 * br1) + (ai0 * bi0 + ai1 * bi1)
        imags[rows, :] = (ai0 * br0 + ai1 * br1) - (ar0 * bi0 + ar1 * bi1)

    def rows_of(first_block):
        blocks = []
        for part in (reals, imags):
            for b in (first_block, first_block + 1):
                low = part[pl.ds(b, STEP_PAIRS, stride=half), :]
                high = part[pl.ds(b + half // 2, STEP_PAIRS, stride=half), :]
                blocks.append((low + high).astype(jnp.bfloat16))
        return jnp.concatenate(blocks, axis=1)

    def send(step):
        rows = pl.ds(pl.multiple_of(step * STEP_PAIRS, STEP_PAIRS), STEP_PAIRS)
        return pltpu.make_async_copy(result.at[rows], out_ref.at[rows], sems.at[step])

    def run(step, carry):
        def some(g, inner):
            for q in range(UNROLL):
                mix(step, g * UNROLL + q)
            return inner

        lax.fori_loop(0, STEP_PAIRS // UNROLL, some, 0)
        even = jnp.dot(rows_of(0), even_ref[...], preferred_element_type=jnp.float32)
        odd = jnp.dot(rows_of(2), odd_ref[...], preferred_element_type=jnp.float32)
        here = pl.ds(pl.multiple_of(step * STEP_PAIRS, STEP_PAIRS), STEP_PAIRS)
        result[here, : POINTS // 2] = even + odd
        result[here, POINTS // 2 :] = even - odd
        send(step).start()
        return carry

    def finish(step, carry):
        send(step).wait()
        return carry

    lax.fori_loop(0, pairs // STEP_PAIRS, run, 0)
    lax.fori_loop(0, pairs // STEP_PAIRS, finish, 0)


def local(records, pair_list, live_blocks):
    columns = lax.axis_size("sta")
    nets = lax.axis_size("grp")
    column = lax.axis_index("sta")
    net = lax.axis_index("grp")
    core = column % 2
    vmem = pl.BlockSpec(memory_space=pltpu.VMEM)
    messages = pl.pallas_call(
        pack_kernel,
        out_shape=jax.ShapeDtypeStruct((columns * PER, LANES), jnp.bfloat16),
        in_specs=[vmem],
        out_specs=vmem,
        compiler_params=pltpu.CompilerParams(vmem_limit_bytes=8 * 2**20),
        cost_estimate=pl.CostEstimate(flops=2 * 10**10, bytes_accessed=3 * 2**17, transcendentals=0),
    )(records.T)
    received = lax.all_to_all(
        messages.reshape(columns, PER, LANES), "sta", split_axis=0, concat_axis=0, tiled=True
    ).reshape(columns * PER, LANES)
    band, share = band_tables()
    size = PER * ROWS
    both, given, other = pl.pallas_call(
        whiten_kernel,
        out_shape=(
            jax.ShapeDtypeStruct((2 * size, LANES), jnp.bfloat16),
            jax.ShapeDtypeStruct((size, LANES), jnp.bfloat16),
            jax.ShapeDtypeStruct((size, LANES), jnp.bfloat16),
        ),
        in_specs=[vmem] * 4,
        out_specs=(vmem, vmem, vmem),
        scratch_shapes=[
            pltpu.VMEM((2 * SEGMENTS * PER, POINTS), jnp.bfloat16),
            pltpu.VMEM((2 * size, LANES), jnp.float32),
        ],
        compiler_params=pltpu.CompilerParams(vmem_limit_bytes=16 * 2**20),
        cost_estimate=pl.CostEstimate(flops=2 * 10**9, bytes_accessed=3 * 2**20, transcendentals=0),
    )(received, jnp.asarray(forward_table()), jnp.asarray(band), jnp.asarray(share))
    def from_net(value, by):
        return lax.ppermute(value, "grp", [((i + by) % nets, i) for i in range(nets)])

    def from_other_core(value):
        return lax.ppermute(value, "sta", [(i, i ^ 1) for i in range(columns)])

    other2, given2 = from_net(other, 2), from_net(given, 2)
    both1, both3 = from_net(both, 1), from_net(both, 3)
    pieces = [both, both1, given2, other2, both3]
    swapped = [from_other_core(part) for part in (given, both1[:size], given2, both3[:size])]

    station_net = pair_list // (columns * PER)
    offset = pair_list // PER % columns - column
    slot = jnp.where(offset == 1, 2, jnp.where(offset == 0, 1 - core, core))
    place = ((slot * nets + (station_net - net) % nets) * PER + pair_list % PER) * ROWS
    in_use = jnp.arange(pair_list.shape[0], dtype=jnp.int32)[:, None, None] < live_blocks[0]
    index = jnp.where(in_use, place, ZERO_ROW).transpose(2, 0, 1).reshape(-1)
    even, odd = lag_tables()
    pairs = pair_list.shape[0] * BLOCK
    steps = pairs // STEP_PAIRS
    return pl.pallas_call(
        pair_kernel,
        out_shape=jax.ShapeDtypeStruct((pairs, POINTS), jnp.float32),
        in_specs=[vmem] * 12,
        out_specs=pl.BlockSpec(memory_space=pl.ANY),
        scratch_shapes=[
            pltpu.VMEM((ZERO_ROW + ROWS, LANES), jnp.float32),
            pltpu.VMEM((STEP_PAIRS * ROWS // 4, LANES), jnp.float32),
            pltpu.VMEM((STEP_PAIRS * ROWS // 4, LANES), jnp.float32),
            pltpu.VMEM((pairs, POINTS), jnp.float32),
            pltpu.SMEM((2 * pairs,), jnp.int32),
            pltpu.SemaphoreType.DMA,
            pltpu.SemaphoreType.DMA((steps,)),
        ],
        compiler_params=pltpu.CompilerParams(vmem_limit_bytes=24 * 2**20),
        cost_estimate=pl.CostEstimate(flops=6 * 10**9, bytes_accessed=6 * 2**20, transcendentals=0),
    )(index, jnp.asarray(even), jnp.asarray(odd), *pieces, *swapped).reshape(
        pair_list.shape[0], BLOCK, POINTS
    )


def solution(mesh):
    in_specs = (P("grp", "sta"), P(("sta", "grp"), None, None), P(("sta", "grp")))
    out_specs = P(("sta", "grp"), None, None)
    return jax.shard_map(local, mesh=mesh, in_specs=in_specs, out_specs=out_specs, check_vma=False)
```

```python
import math

import jax
import jax.numpy as jnp
import ml_dtypes
import numpy as np
from jax import lax
from jax.experimental import pallas as pl
from jax.experimental.pallas import tpu as pltpu
from jax.sharding import PartitionSpec as P

SEGMENTS = 4
POINTS = 1024
BINS = 512
HALF = 16
BLOCK = 128
NETS = 4
PER = 16
SLOTS = 3
ROWS = 32
LANES = 128
STEP_PAIRS = 256
UNROLL = 64
ZERO_ROW = SLOTS * NETS * PER * ROWS

BIN_ORDER = np.concatenate([np.arange(2, BINS + 1, 2), np.arange(1, BINS + 1, 2)])


def forward_table():
    t = np.arange(POINTS, dtype=np.int64)[:, None]
    turn = (t * BIN_ORDER[None, :] % POINTS) * (2.0 * math.pi / POINTS)
    table = np.concatenate([np.cos(turn), -np.sin(turn)], axis=1) / math.sqrt(POINTS)
    return table.astype(np.float32).astype(ml_dtypes.bfloat16)


def lag_tables():
    lag = np.arange(POINTS // 2, dtype=np.int64)[None, :] - POINTS // 2
    tables = []
    for bins in (BIN_ORDER[: BINS // 2], BIN_ORDER[BINS // 2 :]):
        turn = (bins[:, None] * lag % POINTS) * (2.0 * math.pi / POINTS)
        table = np.concatenate([np.cos(turn), -np.sin(turn)], axis=0) / math.sqrt(BINS * SEGMENTS)
        tables.append(table.astype(np.float32).astype(ml_dtypes.bfloat16))
    return tables


def band_tables():
    near = np.abs(BIN_ORDER[:, None] - BIN_ORDER[None, :]) <= HALF
    share = 1.0 / (near.sum(axis=0) * SEGMENTS)
    return near.astype(np.float32).astype(ml_dtypes.bfloat16), share.astype(np.float32)[None, :]


def pack_kernel(records_ref, out_ref):
    samples, stations = records_ref.shape
    own = records_ref[...].astype(jnp.float32)
    ahead = jnp.concatenate([own[:, 2 * PER :], own[:, : 2 * PER]], axis=1)
    both = jnp.concatenate([own, ahead], axis=0)
    for block in range(stations // LANES):
        part = both[:, block * LANES : (block + 1) * LANES]
        out_ref[block * LANES : (block + 1) * LANES, :] = part.T.astype(jnp.bfloat16)


def whiten_kernel(
    parts_ref, forward_ref, band_ref, share_ref, given_ref, other_ref, segs, wide
):
    core = lax.rem(lax.axis_index("sta"), 2)
    low = lax.broadcasted_iota(jnp.int32, (PER, LANES), 1) < LANES // 2
    for e in range(SEGMENTS):
        for u in range(POINTS // LANES):
            row = (e * POINTS // LANES + u) * 2 * PER
            first = parts_ref[row : row + PER, :].astype(jnp.float32)
            second = parts_ref[row + PER : row + 2 * PER, :].astype(jnp.float32)
            near = jnp.where(low, first, pltpu.roll(second, LANES // 2, 1))
            far = jnp.where(low, pltpu.roll(first, LANES // 2, 1), second)
            segs[e * PER : (e + 1) * PER, u * LANES : (u + 1) * LANES] = near.astype(jnp.bfloat16)
            segs[(SEGMENTS + e) * PER : (SEGMENTS + e + 1) * PER, u * LANES : (u + 1) * LANES] = (
                far.astype(jnp.bfloat16)
            )
    spectra = jnp.dot(segs[...], forward_ref[...], preferred_element_type=jnp.float32)
    squares = (spectra * spectra).reshape(2, SEGMENTS, PER, 2 * BINS)
    energy = jnp.sum(squares, axis=1).reshape(2 * PER, 2 * BINS)
    energy = energy[:, :BINS] + energy[:, BINS:]
    top = energy.astype(jnp.bfloat16)
    rest = energy - top.astype(jnp.float32)
    middle = rest.astype(jnp.bfloat16)
    bottom = (rest - middle.astype(jnp.float32)).astype(jnp.bfloat16)
    split = jnp.concatenate([top, middle, bottom], axis=0)
    sums = jnp.dot(split, band_ref[...], preferred_element_type=jnp.float32)
    count = 2 * PER
    total = sums[:count] + (sums[count : 2 * count] + sums[2 * count :])
    scale = lax.rsqrt(total * share_ref[...] + 1e-06)
    for column in range(2):
        for e in range(SEGMENTS):
            for k in range(0, PER, 8):
                for part in range(2):
                    for j in range(BINS // LANES):
                        at = (column * SEGMENTS + e) * PER + k
                        lane = part * BINS + j * LANES
                        piece = (
                            spectra[at : at + 8, lane : lane + LANES]
                            * scale[column * PER + k : column * PER + k + 8, j * LANES : (j + 1) * LANES]
                        )
                        row = (column * PER + k) * ROWS + part * (ROWS // 2) + e * (BINS // LANES) + j
                        wide[pl.ds(row, 8, stride=ROWS), :] = piece
    size = PER * ROWS
    given = 1 - core
    given_ref[...] = wide[pl.ds(pl.multiple_of(given * size, size), size), :].astype(jnp.bfloat16)
    other_ref[...] = wide[pl.ds(pl.multiple_of(core * size, size), size), :].astype(jnp.bfloat16)


def pair_kernel(index_ref, even_ref, odd_ref, *refs):
    sources, (out_ref, *scratch) = refs[: SLOTS * NETS], refs[SLOTS * NETS :]
    table, reals, imags, result, places, place_sem, sems = scratch
    size = PER * ROWS
    half = ROWS // 4
    pairs = index_ref.shape[0] // 2
    load_places = pltpu.make_async_copy(index_ref, places, place_sem)
    load_places.start()
    for n, source in enumerate(sources):
        table[n * size : (n + 1) * size, :] = source[...].astype(jnp.float32)
    table[ZERO_ROW : ZERO_ROW + ROWS, :] = jnp.zeros((ROWS, LANES), jnp.float32)
    load_places.wait()

    def mix(step, q):
        at = step * STEP_PAIRS + q
        first = table[pl.ds(pl.multiple_of(places[at], ROWS), ROWS), :]
        second = table[pl.ds(pl.multiple_of(places[pairs + at], ROWS), ROWS), :]
        ar0, ar1, ai0, ai1 = (first[n : n + half] for n in range(0, ROWS, half))
        br0, br1, bi0, bi1 = (second[n : n + half] for n in range(0, ROWS, half))
        rows = pl.ds(pl.multiple_of(q * half, half), half)
        reals[rows, :] = (ar0 * br0 + ar1 * br1) + (ai0 * bi0 + ai1 * bi1)
        imags[rows, :] = (ai0 * br0 + ai1 * br1) - (ar0 * bi0 + ar1 * bi1)

    def rows_of(first_block):
        blocks = []
        for part in (reals, imags):
            for b in (first_block, first_block + 1):
                low = part[pl.ds(b, STEP_PAIRS, stride=half), :]
                high = part[pl.ds(b + half // 2, STEP_PAIRS, stride=half), :]
                blocks.append((low + high).astype(jnp.bfloat16))
        return jnp.concatenate(blocks, axis=1)

    def send(step):
        rows = pl.ds(pl.multiple_of(step * STEP_PAIRS, STEP_PAIRS), STEP_PAIRS)
        return pltpu.make_async_copy(result.at[rows], out_ref.at[rows], sems.at[step])

    def run(step, carry):
        def some(g, inner):
            for q in range(UNROLL):
                mix(step, g * UNROLL + q)
            return inner

        lax.fori_loop(0, STEP_PAIRS // UNROLL, some, 0)
        even = jnp.dot(rows_of(0), even_ref[...], preferred_element_type=jnp.float32)
        odd = jnp.dot(rows_of(2), odd_ref[...], preferred_element_type=jnp.float32)
        here = pl.ds(pl.multiple_of(step * STEP_PAIRS, STEP_PAIRS), STEP_PAIRS)
        result[here, : POINTS // 2] = even + odd
        result[here, POINTS // 2 :] = even - odd
        send(step).start()
        return carry

    def finish(step, carry):
        send(step).wait()
        return carry

    lax.fori_loop(0, pairs // STEP_PAIRS, run, 0)
    lax.fori_loop(0, pairs // STEP_PAIRS, finish, 0)


def local(records, pair_list, live_blocks):
    columns = lax.axis_size("sta")
    nets = lax.axis_size("grp")
    column = lax.axis_index("sta")
    net = lax.axis_index("grp")
    core = column % 2
    vmem = pl.BlockSpec(memory_space=pltpu.VMEM)
    messages = pl.pallas_call(
        pack_kernel,
        out_shape=jax.ShapeDtypeStruct((columns * PER, LANES), jnp.bfloat16),
        in_specs=[vmem],
        out_specs=vmem,
        compiler_params=pltpu.CompilerParams(vmem_limit_bytes=8 * 2**20),
        cost_estimate=pl.CostEstimate(flops=2 * 10**10, bytes_accessed=3 * 2**17, transcendentals=0),
    )(records.T)
    received = lax.all_to_all(
        messages.reshape(columns, PER, LANES), "sta", split_axis=0, concat_axis=0, tiled=True
    ).reshape(columns * PER, LANES)
    band, share = band_tables()
    size = PER * ROWS
    given, other = pl.pallas_call(
        whiten_kernel,
        out_shape=(
            jax.ShapeDtypeStruct((size, LANES), jnp.bfloat16),
            jax.ShapeDtypeStruct((size, LANES), jnp.bfloat16),
        ),
        in_specs=[vmem] * 4,
        out_specs=(vmem, vmem),
        scratch_shapes=[
            pltpu.VMEM((2 * SEGMENTS * PER, POINTS), jnp.bfloat16),
            pltpu.VMEM((2 * size, LANES), jnp.float32),
        ],
        compiler_params=pltpu.CompilerParams(vmem_limit_bytes=16 * 2**20),
        cost_estimate=pl.CostEstimate(flops=2 * 10**9, bytes_accessed=3 * 2**20, transcendentals=0),
    )(received, jnp.asarray(forward_table()), jnp.asarray(band), jnp.asarray(share))
    def from_net(value, by):
        return lax.ppermute(value, "grp", [((i + by) % nets, i) for i in range(nets)])

    def from_other_core(value):
        return lax.ppermute(value, "sta", [(i, i ^ 1) for i in range(columns)])

    other3, given1 = from_net(other, 3), from_net(given, 1)
    other1, given3 = from_net(other, 1), from_net(given, 3)
    other2, given2 = from_net(other1, 1), from_net(given3, 3)
    first, third, other1 = lax.optimization_barrier((given, given3, other1))
    givens = [given, given1, given2, given3]
    pieces = givens + [other, other1, other2, other3] + [from_other_core(part) for part in (first, given1, given2, third)]

    station_net = pair_list // (columns * PER)
    offset = pair_list // PER % columns - column
    slot = jnp.where(offset == 1, 2, jnp.where(offset == 0, 1 - core, core))
    place = ((slot * nets + (station_net - net) % nets) * PER + pair_list % PER) * ROWS
    in_use = jnp.arange(pair_list.shape[0], dtype=jnp.int32)[:, None, None] < live_blocks[0]
    index = jnp.where(in_use, place, ZERO_ROW).transpose(2, 0, 1).reshape(-1)
    even, odd = lag_tables()
    pairs = pair_list.shape[0] * BLOCK
    steps = pairs // STEP_PAIRS
    return pl.pallas_call(
        pair_kernel,
        out_shape=jax.ShapeDtypeStruct((pairs, POINTS), jnp.float32),
        in_specs=[vmem] * (3 + SLOTS * NETS),
        out_specs=pl.BlockSpec(memory_space=pl.ANY),
        scratch_shapes=[
            pltpu.VMEM((ZERO_ROW + ROWS, LANES), jnp.float32),
            pltpu.VMEM((STEP_PAIRS * ROWS // 4, LANES), jnp.float32),
            pltpu.VMEM((STEP_PAIRS * ROWS // 4, LANES), jnp.float32),
            pltpu.VMEM((pairs, POINTS), jnp.float32),
            pltpu.SMEM((2 * pairs,), jnp.int32),
            pltpu.SemaphoreType.DMA,
            pltpu.SemaphoreType.DMA((steps,)),
        ],
        compiler_params=pltpu.CompilerParams(vmem_limit_bytes=24 * 2**20),
        cost_estimate=pl.CostEstimate(flops=6 * 10**9, bytes_accessed=6 * 2**20, transcendentals=0),
    )(index, jnp.asarray(even), jnp.asarray(odd), *pieces).reshape(
        pair_list.shape[0], BLOCK, POINTS
    )


def solution(mesh):
    in_specs = (P("grp", "sta"), P(("sta", "grp"), None, None), P(("sta", "grp")))
    out_specs = P(("sta", "grp"), None, None)
    return jax.shard_map(local, mesh=mesh, in_specs=in_specs, out_specs=out_specs, check_vma=False)
```

```python
import math

import jax
import jax.numpy as jnp
import ml_dtypes
import numpy as np
from jax import lax
from jax.experimental import pallas as pl
from jax.experimental.pallas import tpu as pltpu
from jax.sharding import PartitionSpec as P

SEGMENTS = 4
POINTS = 1024
BINS = 512
HALF = 16
BLOCK = 128
NETS = 4
PER = 16
SLOTS = 3
ROWS = 32
LANES = 128
STEP_PAIRS = 256
UNROLL = 64
ZERO_ROW = SLOTS * NETS * PER * ROWS

BIN_ORDER = np.concatenate([np.arange(2, BINS + 1, 2), np.arange(1, BINS + 1, 2)])


def forward_table():
    t = np.arange(POINTS, dtype=np.int64)[:, None]
    turn = (t * BIN_ORDER[None, :] % POINTS) * (2.0 * math.pi / POINTS)
    table = np.concatenate([np.cos(turn), -np.sin(turn)], axis=1) / math.sqrt(POINTS)
    return table.astype(np.float32).astype(ml_dtypes.bfloat16)


def lag_tables():
    lag = np.arange(POINTS // 2, dtype=np.int64)[None, :] - POINTS // 2
    tables = []
    for bins in (BIN_ORDER[: BINS // 2], BIN_ORDER[BINS // 2 :]):
        turn = (bins[:, None] * lag % POINTS) * (2.0 * math.pi / POINTS)
        table = np.concatenate([np.cos(turn), -np.sin(turn)], axis=0) / math.sqrt(BINS * SEGMENTS)
        tables.append(table.astype(np.float32).astype(ml_dtypes.bfloat16))
    return tables


def band_tables():
    near = np.abs(BIN_ORDER[:, None] - BIN_ORDER[None, :]) <= HALF
    share = 1.0 / (near.sum(axis=0) * SEGMENTS)
    return near.astype(np.float32).astype(ml_dtypes.bfloat16), share.astype(np.float32)[None, :]


def pack_kernel(records_ref, out_ref):
    samples, stations = records_ref.shape
    own = records_ref[...].astype(jnp.float32)
    ahead = jnp.concatenate([own[:, 2 * PER :], own[:, : 2 * PER]], axis=1)
    both = jnp.concatenate([own, ahead], axis=0)
    for block in range(stations // LANES):
        part = both[:, block * LANES : (block + 1) * LANES]
        out_ref[block * LANES : (block + 1) * LANES, :] = part.T.astype(jnp.bfloat16)


def whiten_kernel(
    parts_ref, forward_ref, band_ref, share_ref, given_ref, other_ref, segs, wide
):
    core = lax.rem(lax.axis_index("sta"), 2)
    low = lax.broadcasted_iota(jnp.int32, (PER, LANES), 1) < LANES // 2
    for e in range(SEGMENTS):
        for u in range(POINTS // LANES):
            row = (e * POINTS // LANES + u) * 2 * PER
            first = parts_ref[row : row + PER, :].astype(jnp.float32)
            second = parts_ref[row + PER : row + 2 * PER, :].astype(jnp.float32)
            near = jnp.where(low, first, pltpu.roll(second, LANES // 2, 1))
            far = jnp.where(low, pltpu.roll(first, LANES // 2, 1), second)
            segs[e * PER : (e + 1) * PER, u * LANES : (u + 1) * LANES] = near.astype(jnp.bfloat16)
            segs[(SEGMENTS + e) * PER : (SEGMENTS + e + 1) * PER, u * LANES : (u + 1) * LANES] = (
                far.astype(jnp.bfloat16)
            )
    spectra = jnp.dot(segs[...], forward_ref[...], preferred_element_type=jnp.float32)
    squares = (spectra * spectra).reshape(2, SEGMENTS, PER, 2 * BINS)
    energy = jnp.sum(squares, axis=1).reshape(2 * PER, 2 * BINS)
    energy = energy[:, :BINS] + energy[:, BINS:]
    top = energy.astype(jnp.bfloat16)
    rest = energy - top.astype(jnp.float32)
    middle = rest.astype(jnp.bfloat16)
    bottom = (rest - middle.astype(jnp.float32)).astype(jnp.bfloat16)
    split = jnp.concatenate([top, middle, bottom], axis=0)
    sums = jnp.dot(split, band_ref[...], preferred_element_type=jnp.float32)
    count = 2 * PER
    total = sums[:count] + (sums[count : 2 * count] + sums[2 * count :])
    scale = lax.rsqrt(total * share_ref[...] + 1e-06)
    for column in range(2):
        for e in range(SEGMENTS):
            for k in range(0, PER, 8):
                for part in range(2):
                    for j in range(BINS // LANES):
                        at = (column * SEGMENTS + e) * PER + k
                        lane = part * BINS + j * LANES
                        piece = (
                            spectra[at : at + 8, lane : lane + LANES]
                            * scale[column * PER + k : column * PER + k + 8, j * LANES : (j + 1) * LANES]
                        )
                        row = (column * PER + k) * ROWS + part * (ROWS // 2) + e * (BINS // LANES) + j
                        wide[pl.ds(row, 8, stride=ROWS), :] = piece
    size = PER * ROWS
    given = 1 - core
    given_ref[...] = wide[pl.ds(pl.multiple_of(given * size, size), size), :].astype(jnp.bfloat16)
    other_ref[...] = wide[pl.ds(pl.multiple_of(core * size, size), size), :].astype(jnp.bfloat16)


def pair_kernel(live_ref, index_ref, even_ref, odd_ref, *refs):
    sources, (out_ref, *scratch) = refs[: SLOTS * NETS], refs[SLOTS * NETS :]
    table, reals, imags, result, places, place_sem, sems = scratch
    size = PER * ROWS
    half = ROWS // 4
    pairs = index_ref.shape[0] // 2
    load_places = pltpu.make_async_copy(index_ref, places, place_sem)
    load_places.start()
    steps = pairs // STEP_PAIRS
    busy = jnp.minimum(lax.div(live_ref[0] * BLOCK + STEP_PAIRS - 1, STEP_PAIRS), steps)

    def rows_at(step):
        return pl.ds(pl.multiple_of(step * STEP_PAIRS, STEP_PAIRS), STEP_PAIRS)

    def send(step):
        rows = rows_at(step)
        return pltpu.make_async_copy(result.at[rows], out_ref.at[rows], sems.at[step])

    def clear(step, carry):
        result[rows_at(step), :] = jnp.zeros((STEP_PAIRS, POINTS), jnp.float32)
        send(step).start()
        return carry

    lax.fori_loop(busy, steps, clear, 0)
    for n, source in enumerate(sources):
        table[n * size : (n + 1) * size, :] = source[...].astype(jnp.float32)
    table[ZERO_ROW : ZERO_ROW + ROWS, :] = jnp.zeros((ROWS, LANES), jnp.float32)
    load_places.wait()

    def mix(step, q):
        at = step * STEP_PAIRS + q
        first = table[pl.ds(pl.multiple_of(places[at], ROWS), ROWS), :]
        second = table[pl.ds(pl.multiple_of(places[pairs + at], ROWS), ROWS), :]
        ar0, ar1, ai0, ai1 = (first[n : n + half] for n in range(0, ROWS, half))
        br0, br1, bi0, bi1 = (second[n : n + half] for n in range(0, ROWS, half))
        rows = pl.ds(pl.multiple_of(q * half, half), half)
        reals[rows, :] = (ar0 * br0 + ar1 * br1) + (ai0 * bi0 + ai1 * bi1)
        imags[rows, :] = (ai0 * br0 + ai1 * br1) - (ar0 * bi0 + ar1 * bi1)

    def rows_of(first_block):
        blocks = []
        for part in (reals, imags):
            for b in (first_block, first_block + 1):
                low = part[pl.ds(b, STEP_PAIRS, stride=half), :]
                high = part[pl.ds(b + half // 2, STEP_PAIRS, stride=half), :]
                blocks.append((low + high).astype(jnp.bfloat16))
        return jnp.concatenate(blocks, axis=1)

    def run(step, carry):
        def some(g, inner):
            for q in range(UNROLL):
                mix(step, g * UNROLL + q)
            return inner

        lax.fori_loop(0, STEP_PAIRS // UNROLL, some, 0)
        even = jnp.dot(rows_of(0), even_ref[...], preferred_element_type=jnp.float32)
        odd = jnp.dot(rows_of(2), odd_ref[...], preferred_element_type=jnp.float32)
        here = rows_at(step)
        result[here, : POINTS // 2] = even + odd
        result[here, POINTS // 2 :] = even - odd
        send(step).start()
        return carry

    def finish(step, carry):
        send(step).wait()
        return carry

    lax.fori_loop(0, busy, run, 0)
    lax.fori_loop(0, steps, finish, 0)


def local(records, pair_list, live_blocks):
    columns = lax.axis_size("sta")
    nets = lax.axis_size("grp")
    column = lax.axis_index("sta")
    net = lax.axis_index("grp")
    core = column % 2
    vmem = pl.BlockSpec(memory_space=pltpu.VMEM)
    messages = pl.pallas_call(
        pack_kernel,
        out_shape=jax.ShapeDtypeStruct((columns * PER, LANES), jnp.bfloat16),
        in_specs=[vmem],
        out_specs=vmem,
        compiler_params=pltpu.CompilerParams(vmem_limit_bytes=8 * 2**20),
        cost_estimate=pl.CostEstimate(flops=2 * 10**10, bytes_accessed=3 * 2**17, transcendentals=0),
    )(records.T)
    received = lax.all_to_all(
        messages.reshape(columns, PER, LANES), "sta", split_axis=0, concat_axis=0, tiled=True
    ).reshape(columns * PER, LANES)
    band, share = band_tables()
    size = PER * ROWS
    given, other = pl.pallas_call(
        whiten_kernel,
        out_shape=(
            jax.ShapeDtypeStruct((size, LANES), jnp.bfloat16),
            jax.ShapeDtypeStruct((size, LANES), jnp.bfloat16),
        ),
        in_specs=[vmem] * 4,
        out_specs=(vmem, vmem),
        scratch_shapes=[
            pltpu.VMEM((2 * SEGMENTS * PER, POINTS), jnp.bfloat16),
            pltpu.VMEM((2 * size, LANES), jnp.float32),
        ],
        compiler_params=pltpu.CompilerParams(vmem_limit_bytes=16 * 2**20),
        cost_estimate=pl.CostEstimate(flops=2 * 10**9, bytes_accessed=3 * 2**20, transcendentals=0),
    )(received, jnp.asarray(forward_table()), jnp.asarray(band), jnp.asarray(share))
    def from_net(value, by):
        return lax.ppermute(value, "grp", [((i + by) % nets, i) for i in range(nets)])

    def from_other_core(value):
        return lax.ppermute(value, "sta", [(i, i ^ 1) for i in range(columns)])

    other3, given1 = from_net(other, 3), from_net(given, 1)
    other1, given3 = from_net(other, 1), from_net(given, 3)
    other2, given2 = from_net(other1, 1), from_net(given3, 3)
    first, third, other1 = lax.optimization_barrier((given, given3, other1))
    givens = [given, given1, given2, given3]
    pieces = givens + [other, other1, other2, other3] + [from_other_core(part) for part in (first, given1, given2, third)]

    station_net = pair_list // (columns * PER)
    offset = pair_list // PER % columns - column
    slot = jnp.where(offset == 1, 2, jnp.where(offset == 0, 1 - core, core))
    place = ((slot * nets + (station_net - net) % nets) * PER + pair_list % PER) * ROWS
    in_use = jnp.arange(pair_list.shape[0], dtype=jnp.int32)[:, None, None] < live_blocks[0]
    index = jnp.where(in_use, place, ZERO_ROW).transpose(2, 0, 1).reshape(-1)
    even, odd = lag_tables()
    pairs = pair_list.shape[0] * BLOCK
    steps = pairs // STEP_PAIRS
    return pl.pallas_call(
        pair_kernel,
        out_shape=jax.ShapeDtypeStruct((pairs, POINTS), jnp.float32),
        in_specs=[pl.BlockSpec(memory_space=pltpu.SMEM)] + [vmem] * (3 + SLOTS * NETS),
        out_specs=pl.BlockSpec(memory_space=pl.ANY),
        scratch_shapes=[
            pltpu.VMEM((ZERO_ROW + ROWS, LANES), jnp.float32),
            pltpu.VMEM((STEP_PAIRS * ROWS // 4, LANES), jnp.float32),
            pltpu.VMEM((STEP_PAIRS * ROWS // 4, LANES), jnp.float32),
            pltpu.VMEM((pairs, POINTS), jnp.float32),
            pltpu.SMEM((2 * pairs,), jnp.int32),
            pltpu.SemaphoreType.DMA,
            pltpu.SemaphoreType.DMA((steps,)),
        ],
        compiler_params=pltpu.CompilerParams(vmem_limit_bytes=24 * 2**20),
        cost_estimate=pl.CostEstimate(flops=6 * 10**9, bytes_accessed=6 * 2**20, transcendentals=0),
    )(live_blocks, index, jnp.asarray(even), jnp.asarray(odd), *pieces).reshape(
        pair_list.shape[0], BLOCK, POINTS
    )


def solution(mesh):
    in_specs = (P("grp", "sta"), P(("sta", "grp"), None, None), P(("sta", "grp")))
    out_specs = P(("sta", "grp"), None, None)
    return jax.shard_map(local, mesh=mesh, in_specs=in_specs, out_specs=out_specs, check_vma=False)
```

```python
import math

import jax
import jax.numpy as jnp
import ml_dtypes
import numpy as np
from jax import lax
from jax.experimental import pallas as pl
from jax.experimental.pallas import tpu as pltpu
from jax.sharding import PartitionSpec as P

SEGMENTS = 4
POINTS = 1024
BINS = 512
HALF = 16
BLOCK = 128
NETS = 4
PER = 16
SLOTS = 3
ROWS = 32
LANES = 128
STEP_PAIRS = 256
UNROLL = 64

BIN_ORDER = np.concatenate([np.arange(2, BINS + 1, 2), np.arange(1, BINS + 1, 2)])


def forward_table():
    t = np.arange(POINTS, dtype=np.int64)[:, None]
    turn = (t * BIN_ORDER[None, :] % POINTS) * (2.0 * math.pi / POINTS)
    table = np.concatenate([np.cos(turn), -np.sin(turn)], axis=1) / math.sqrt(POINTS)
    return table.astype(np.float32).astype(ml_dtypes.bfloat16)


def lag_tables():
    lag = np.arange(POINTS // 2, dtype=np.int64)[None, :] - POINTS // 2
    tables = []
    for bins in (BIN_ORDER[: BINS // 2], BIN_ORDER[BINS // 2 :]):
        turn = (bins[:, None] * lag % POINTS) * (2.0 * math.pi / POINTS)
        table = np.concatenate([np.cos(turn), -np.sin(turn)], axis=0) / math.sqrt(BINS * SEGMENTS)
        tables.append(table.astype(np.float32).astype(ml_dtypes.bfloat16))
    return tables


def band_tables():
    near = np.abs(BIN_ORDER[:, None] - BIN_ORDER[None, :]) <= HALF
    share = 1.0 / (near.sum(axis=0) * SEGMENTS)
    return near.astype(np.float32).astype(ml_dtypes.bfloat16), share.astype(np.float32)[None, :]


def pack_kernel(records_ref, out_ref):
    samples, stations = records_ref.shape
    own = records_ref[...].astype(jnp.float32)
    ahead = jnp.concatenate([own[:, 2 * PER :], own[:, : 2 * PER]], axis=1)
    both = jnp.concatenate([own, ahead], axis=0)
    for block in range(stations // LANES):
        part = both[:, block * LANES : (block + 1) * LANES]
        out_ref[block * LANES : (block + 1) * LANES, :] = part.T.astype(jnp.bfloat16)


def whiten_kernel(
    parts_ref, forward_ref, band_ref, share_ref, given_ref, other_ref, segs, wide
):
    core = lax.rem(lax.axis_index("sta"), 2)
    low = lax.broadcasted_iota(jnp.int32, (PER, LANES), 1) < LANES // 2
    for e in range(SEGMENTS):
        for u in range(POINTS // LANES):
            row = (e * POINTS // LANES + u) * 2 * PER
            first = parts_ref[row : row + PER, :].astype(jnp.float32)
            second = parts_ref[row + PER : row + 2 * PER, :].astype(jnp.float32)
            near = jnp.where(low, first, pltpu.roll(second, LANES // 2, 1))
            far = jnp.where(low, pltpu.roll(first, LANES // 2, 1), second)
            segs[e * PER : (e + 1) * PER, u * LANES : (u + 1) * LANES] = near.astype(jnp.bfloat16)
            segs[(SEGMENTS + e) * PER : (SEGMENTS + e + 1) * PER, u * LANES : (u + 1) * LANES] = (
                far.astype(jnp.bfloat16)
            )
    spectra = jnp.dot(segs[...], forward_ref[...], preferred_element_type=jnp.float32)
    squares = (spectra * spectra).reshape(2, SEGMENTS, PER, 2 * BINS)
    energy = jnp.sum(squares, axis=1).reshape(2 * PER, 2 * BINS)
    energy = energy[:, :BINS] + energy[:, BINS:]
    top = energy.astype(jnp.bfloat16)
    rest = energy - top.astype(jnp.float32)
    middle = rest.astype(jnp.bfloat16)
    bottom = (rest - middle.astype(jnp.float32)).astype(jnp.bfloat16)
    split = jnp.concatenate([top, middle, bottom], axis=0)
    sums = jnp.dot(split, band_ref[...], preferred_element_type=jnp.float32)
    count = 2 * PER
    total = sums[:count] + (sums[count : 2 * count] + sums[2 * count :])
    scale = lax.rsqrt(total * share_ref[...] + 1e-06)
    for column in range(2):
        for e in range(SEGMENTS):
            for k in range(0, PER, 8):
                for part in range(2):
                    for j in range(BINS // LANES):
                        at = (column * SEGMENTS + e) * PER + k
                        lane = part * BINS + j * LANES
                        piece = (
                            spectra[at : at + 8, lane : lane + LANES]
                            * scale[column * PER + k : column * PER + k + 8, j * LANES : (j + 1) * LANES]
                        )
                        row = (column * PER + k) * ROWS + part * (ROWS // 2) + e * (BINS // LANES) + j
                        wide[pl.ds(row, 8, stride=ROWS), :] = piece
    size = PER * ROWS
    given = 1 - core
    given_ref[...] = wide[pl.ds(pl.multiple_of(given * size, size), size), :].astype(jnp.bfloat16)
    other_ref[...] = wide[pl.ds(pl.multiple_of(core * size, size), size), :].astype(jnp.bfloat16)


def pair_kernel(live_ref, index_ref, even_ref, odd_ref, *refs):
    sources, (out_ref, *scratch) = refs[: SLOTS * NETS], refs[SLOTS * NETS :]
    table, reals, imags, result, places, place_sem, sems, block_sems = scratch
    size = PER * ROWS
    half = ROWS // 4
    pairs = index_ref.shape[0] // 2
    load_places = pltpu.make_async_copy(index_ref, places, place_sem)
    load_places.start()
    live = jnp.minimum(live_ref[0], pairs // BLOCK)
    full = lax.div(live, STEP_PAIRS // BLOCK)

    def send(step, count, which):
        rows = pl.ds(pl.multiple_of(step * count, count), count)
        return pltpu.make_async_copy(result.at[rows], out_ref.at[rows], which.at[step])

    def clear(block, carry):
        rows = pl.ds(pl.multiple_of(block * BLOCK, BLOCK), BLOCK)
        result[rows, :] = jnp.zeros((BLOCK, POINTS), jnp.float32)
        send(block, BLOCK, block_sems).start()
        return carry

    lax.fori_loop(live, pairs // BLOCK, clear, 0)
    for n, source in enumerate(sources):
        table[n * size : (n + 1) * size, :] = source[...].astype(jnp.float32)
    load_places.wait()

    def mix(first_pair, q):
        at = first_pair + q
        first = table[pl.ds(pl.multiple_of(places[at], ROWS), ROWS), :]
        second = table[pl.ds(pl.multiple_of(places[pairs + at], ROWS), ROWS), :]
        ar0, ar1, ai0, ai1 = (first[n : n + half] for n in range(0, ROWS, half))
        br0, br1, bi0, bi1 = (second[n : n + half] for n in range(0, ROWS, half))
        rows = pl.ds(pl.multiple_of(q * half, half), half)
        reals[rows, :] = (ar0 * br0 + ar1 * br1) + (ai0 * bi0 + ai1 * bi1)
        imags[rows, :] = (ai0 * br0 + ai1 * br1) - (ar0 * bi0 + ar1 * bi1)

    def rows_of(first_block, count):
        blocks = []
        for part in (reals, imags):
            for b in (first_block, first_block + 1):
                low = part[pl.ds(b, count, stride=half), :]
                high = part[pl.ds(b + half // 2, count, stride=half), :]
                blocks.append((low + high).astype(jnp.bfloat16))
        return jnp.concatenate(blocks, axis=1)

    def work(step, count, which):
        def some(g, inner):
            for q in range(UNROLL):
                mix(step * count, g * UNROLL + q)
            return inner

        lax.fori_loop(0, count // UNROLL, some, 0)
        even = jnp.dot(rows_of(0, count), even_ref[...], preferred_element_type=jnp.float32)
        odd = jnp.dot(rows_of(2, count), odd_ref[...], preferred_element_type=jnp.float32)
        here = pl.ds(pl.multiple_of(step * count, count), count)
        result[here, : POINTS // 2] = even + odd
        result[here, POINTS // 2 :] = even - odd
        send(step, count, which).start()

    def run(step, carry):
        work(step, STEP_PAIRS, sems)
        return carry

    def finish(step, carry):
        send(step, STEP_PAIRS, sems).wait()
        return carry

    def finish_block(block, carry):
        send(block, BLOCK, block_sems).wait()
        return carry

    lax.fori_loop(0, full, run, 0)

    @pl.when(full * (STEP_PAIRS // BLOCK) < live)
    def _():
        work(live - 1, BLOCK, block_sems)

    lax.fori_loop(0, full, finish, 0)
    lax.fori_loop(full * (STEP_PAIRS // BLOCK), pairs // BLOCK, finish_block, 0)


def local(records, pair_list, live_blocks):
    columns = lax.axis_size("sta")
    nets = lax.axis_size("grp")
    column = lax.axis_index("sta")
    net = lax.axis_index("grp")
    core = column % 2
    vmem = pl.BlockSpec(memory_space=pltpu.VMEM)
    messages = pl.pallas_call(
        pack_kernel,
        out_shape=jax.ShapeDtypeStruct((columns * PER, LANES), jnp.bfloat16),
        in_specs=[vmem],
        out_specs=vmem,
        compiler_params=pltpu.CompilerParams(vmem_limit_bytes=8 * 2**20),
        cost_estimate=pl.CostEstimate(flops=2 * 10**10, bytes_accessed=3 * 2**17, transcendentals=0),
    )(records.T)
    received = lax.all_to_all(
        messages.reshape(columns, PER, LANES), "sta", split_axis=0, concat_axis=0, tiled=True
    ).reshape(columns * PER, LANES)
    band, share = band_tables()
    size = PER * ROWS
    given, other = pl.pallas_call(
        whiten_kernel,
        out_shape=(
            jax.ShapeDtypeStruct((size, LANES), jnp.bfloat16),
            jax.ShapeDtypeStruct((size, LANES), jnp.bfloat16),
        ),
        in_specs=[vmem] * 4,
        out_specs=(vmem, vmem),
        scratch_shapes=[
            pltpu.VMEM((2 * SEGMENTS * PER, POINTS), jnp.bfloat16),
            pltpu.VMEM((2 * size, LANES), jnp.float32),
        ],
        compiler_params=pltpu.CompilerParams(vmem_limit_bytes=16 * 2**20),
        cost_estimate=pl.CostEstimate(flops=2 * 10**9, bytes_accessed=3 * 2**20, transcendentals=0),
    )(received, jnp.asarray(forward_table()), jnp.asarray(band), jnp.asarray(share))
    def from_net(value, by):
        return lax.ppermute(value, "grp", [((i + by) % nets, i) for i in range(nets)])

    def from_other_core(value):
        return lax.ppermute(value, "sta", [(i, i ^ 1) for i in range(columns)])

    other3, given1 = from_net(other, 3), from_net(given, 1)
    other1, given3 = from_net(other, 1), from_net(given, 3)
    other2, given2 = from_net(other1, 1), from_net(given3, 3)
    first, third, other1 = lax.optimization_barrier((given, given3, other1))
    givens = [given, given1, given2, given3]
    pieces = givens + [other, other1, other2, other3] + [from_other_core(part) for part in (first, given1, given2, third)]

    station_net = pair_list // (columns * PER)
    offset = pair_list // PER % columns - column
    slot = jnp.where(offset == 1, 2, jnp.where(offset == 0, 1 - core, core))
    place = ((slot * nets + (station_net - net) % nets) * PER + pair_list % PER) * ROWS
    index = place.transpose(2, 0, 1).reshape(-1)
    even, odd = lag_tables()
    pairs = pair_list.shape[0] * BLOCK
    steps = pairs // STEP_PAIRS
    return pl.pallas_call(
        pair_kernel,
        out_shape=jax.ShapeDtypeStruct((pairs, POINTS), jnp.float32),
        in_specs=[pl.BlockSpec(memory_space=pltpu.SMEM)] + [vmem] * (3 + SLOTS * NETS),
        out_specs=pl.BlockSpec(memory_space=pl.ANY),
        scratch_shapes=[
            pltpu.VMEM((SLOTS * NETS * PER * ROWS, LANES), jnp.float32),
            pltpu.VMEM((STEP_PAIRS * ROWS // 4, LANES), jnp.float32),
            pltpu.VMEM((STEP_PAIRS * ROWS // 4, LANES), jnp.float32),
            pltpu.VMEM((pairs, POINTS), jnp.float32),
            pltpu.SMEM((2 * pairs,), jnp.int32),
            pltpu.SemaphoreType.DMA,
            pltpu.SemaphoreType.DMA((steps,)),
            pltpu.SemaphoreType.DMA((pairs // BLOCK,)),
        ],
        compiler_params=pltpu.CompilerParams(vmem_limit_bytes=24 * 2**20),
        cost_estimate=pl.CostEstimate(flops=6 * 10**9, bytes_accessed=6 * 2**20, transcendentals=0),
    )(live_blocks, index, jnp.asarray(even), jnp.asarray(odd), *pieces).reshape(
        pair_list.shape[0], BLOCK, POINTS
    )


def solution(mesh):
    in_specs = (P("grp", "sta"), P(("sta", "grp"), None, None), P(("sta", "grp")))
    out_specs = P(("sta", "grp"), None, None)
    return jax.shard_map(local, mesh=mesh, in_specs=in_specs, out_specs=out_specs, check_vma=False)
```

```python
import math

import jax
import jax.numpy as jnp
import ml_dtypes
import numpy as np
from jax import lax
from jax.experimental import pallas as pl
from jax.experimental.pallas import tpu as pltpu
from jax.sharding import PartitionSpec as P

SEGMENTS = 4
POINTS = 1024
BINS = 512
HALF = 16
BLOCK = 128
NETS = 4
PER = 16
SLOTS = 3
ROWS = 32
LANES = 128
STEP_PAIRS = 256

BIN_ORDER = np.concatenate([np.arange(2, BINS + 1, 2), np.arange(1, BINS + 1, 2)])


def forward_table():
    t = np.arange(POINTS, dtype=np.int64)[:, None]
    turn = (t * BIN_ORDER[None, :] % POINTS) * (2.0 * math.pi / POINTS)
    table = np.concatenate([np.cos(turn), -np.sin(turn)], axis=1) / math.sqrt(POINTS)
    return table.astype(np.float32).astype(ml_dtypes.bfloat16)


def lag_tables():
    lag = np.arange(POINTS // 2, dtype=np.int64)[None, :] - POINTS // 2
    tables = []
    for bins in (BIN_ORDER[: BINS // 2], BIN_ORDER[BINS // 2 :]):
        turn = (bins[:, None] * lag % POINTS) * (2.0 * math.pi / POINTS)
        table = np.concatenate([np.cos(turn), -np.sin(turn)], axis=0) / math.sqrt(BINS * SEGMENTS)
        tables.append(table.astype(np.float32).astype(ml_dtypes.bfloat16))
    return tables


def band_tables():
    near = np.abs(BIN_ORDER[:, None] - BIN_ORDER[None, :]) <= HALF
    share = 1.0 / (near.sum(axis=0) * SEGMENTS)
    return near.astype(np.float32).astype(ml_dtypes.bfloat16), share.astype(np.float32)[None, :]


def pack_kernel(records_ref, out_ref):
    samples, stations = records_ref.shape
    own = records_ref[...].astype(jnp.float32)
    ahead = jnp.concatenate([own[:, 2 * PER :], own[:, : 2 * PER]], axis=1)
    both = jnp.concatenate([own, ahead], axis=0)
    for block in range(stations // LANES):
        part = both[:, block * LANES : (block + 1) * LANES]
        out_ref[block * LANES : (block + 1) * LANES, :] = part.T.astype(jnp.bfloat16)


def whiten_kernel(
    parts_ref, forward_ref, band_ref, share_ref, given_ref, other_ref, segs, wide
):
    core = lax.rem(lax.axis_index("sta"), 2)
    low = lax.broadcasted_iota(jnp.int32, (PER, LANES), 1) < LANES // 2
    for e in range(SEGMENTS):
        for u in range(POINTS // LANES):
            row = (e * POINTS // LANES + u) * 2 * PER
            first = parts_ref[row : row + PER, :].astype(jnp.float32)
            second = parts_ref[row + PER : row + 2 * PER, :].astype(jnp.float32)
            near = jnp.where(low, first, pltpu.roll(second, LANES // 2, 1))
            far = jnp.where(low, pltpu.roll(first, LANES // 2, 1), second)
            segs[e * PER : (e + 1) * PER, u * LANES : (u + 1) * LANES] = near.astype(jnp.bfloat16)
            segs[(SEGMENTS + e) * PER : (SEGMENTS + e + 1) * PER, u * LANES : (u + 1) * LANES] = (
                far.astype(jnp.bfloat16)
            )
    spectra = jnp.dot(segs[...], forward_ref[...], preferred_element_type=jnp.float32)
    squares = (spectra * spectra).reshape(2, SEGMENTS, PER, 2 * BINS)
    energy = jnp.sum(squares, axis=1).reshape(2 * PER, 2 * BINS)
    energy = energy[:, :BINS] + energy[:, BINS:]
    top = energy.astype(jnp.bfloat16)
    rest = energy - top.astype(jnp.float32)
    middle = rest.astype(jnp.bfloat16)
    bottom = (rest - middle.astype(jnp.float32)).astype(jnp.bfloat16)
    split = jnp.concatenate([top, middle, bottom], axis=0)
    sums = jnp.dot(split, band_ref[...], preferred_element_type=jnp.float32)
    count = 2 * PER
    total = sums[:count] + (sums[count : 2 * count] + sums[2 * count :])
    scale = lax.rsqrt(total * share_ref[...] + 1e-06)
    for column in range(2):
        for e in range(SEGMENTS):
            for k in range(0, PER, 8):
                for part in range(2):
                    for j in range(BINS // LANES):
                        at = (column * SEGMENTS + e) * PER + k
                        lane = part * BINS + j * LANES
                        piece = (
                            spectra[at : at + 8, lane : lane + LANES]
                            * scale[column * PER + k : column * PER + k + 8, j * LANES : (j + 1) * LANES]
                        )
                        row = (column * PER + k) * ROWS + part * (ROWS // 2) + e * (BINS // LANES) + j
                        wide[pl.ds(row, 8, stride=ROWS), :] = piece
    size = PER * ROWS
    given = 1 - core
    given_ref[...] = wide[pl.ds(pl.multiple_of(given * size, size), size), :].astype(jnp.bfloat16)
    other_ref[...] = wide[pl.ds(pl.multiple_of(core * size, size), size), :].astype(jnp.bfloat16)


def pair_kernel(live_ref, index_ref, even_ref, odd_ref, *refs):
    sources, (out_ref, *scratch) = refs[: SLOTS * NETS], refs[SLOTS * NETS :]
    table, reals, imags, result, places, place_sem, sems, block_sems = scratch
    size = PER * ROWS
    half = ROWS // 4
    pairs = index_ref.shape[0] // 2
    load_places = pltpu.make_async_copy(index_ref, places, place_sem)
    load_places.start()
    live = jnp.minimum(live_ref[0], pairs // BLOCK)
    full = lax.div(live, STEP_PAIRS // BLOCK)

    def send(step, count, which):
        rows = pl.ds(pl.multiple_of(step * count, count), count)
        return pltpu.make_async_copy(result.at[rows], out_ref.at[rows], which.at[step])

    def clear(block, carry):
        rows = pl.ds(pl.multiple_of(block * BLOCK, BLOCK), BLOCK)
        result[rows, :] = jnp.zeros((BLOCK, POINTS), jnp.float32)
        send(block, BLOCK, block_sems).start()
        return carry

    lax.fori_loop(live, pairs // BLOCK, clear, 0)
    for n, source in enumerate(sources):
        table[n * size : (n + 1) * size, :] = source[...].astype(jnp.float32)
    load_places.wait()

    def mix(first_pair, q):
        at = first_pair + q
        first = table[pl.ds(pl.multiple_of(places[at], ROWS), ROWS), :]
        second = table[pl.ds(pl.multiple_of(places[pairs + at], ROWS), ROWS), :]
        ar0, ar1, ai0, ai1 = (first[n : n + half] for n in range(0, ROWS, half))
        br0, br1, bi0, bi1 = (second[n : n + half] for n in range(0, ROWS, half))
        rows = pl.ds(pl.multiple_of(q * half, half), half)
        reals[rows, :] = (ar0 * br0 + ar1 * br1) + (ai0 * bi0 + ai1 * bi1)
        imags[rows, :] = (ai0 * br0 + ai1 * br1) - (ar0 * bi0 + ar1 * bi1)

    def rows_of(first_block, count):
        blocks = []
        for part in (reals, imags):
            for b in (first_block, first_block + 1):
                low = part[pl.ds(b, count, stride=half), :]
                high = part[pl.ds(b + half // 2, count, stride=half), :]
                blocks.append((low + high).astype(jnp.bfloat16))
        return jnp.concatenate(blocks, axis=1)

    def work(step, count, which):
        unroll = count // 2

        def some(g, inner):
            for q in range(unroll):
                mix(step * count, g * unroll + q)
            return inner

        lax.fori_loop(0, count // unroll, some, 0)
        even = jnp.dot(rows_of(0, count), even_ref[...], preferred_element_type=jnp.float32)
        odd = jnp.dot(rows_of(2, count), odd_ref[...], preferred_element_type=jnp.float32)
        here = pl.ds(pl.multiple_of(step * count, count), count)
        result[here, : POINTS // 2] = even + odd
        result[here, POINTS // 2 :] = even - odd
        send(step, count, which).start()

    def run(step, carry):
        work(step, STEP_PAIRS, sems)
        return carry

    def finish(step, carry):
        send(step, STEP_PAIRS, sems).wait()
        return carry

    def finish_block(block, carry):
        send(block, BLOCK, block_sems).wait()
        return carry

    lax.fori_loop(0, full, run, 0)

    @pl.when(full * (STEP_PAIRS // BLOCK) < live)
    def _():
        work(live - 1, BLOCK, block_sems)

    lax.fori_loop(0, full, finish, 0)
    lax.fori_loop(full * (STEP_PAIRS // BLOCK), pairs // BLOCK, finish_block, 0)


def local(records, pair_list, live_blocks):
    columns = lax.axis_size("sta")
    nets = lax.axis_size("grp")
    column = lax.axis_index("sta")
    net = lax.axis_index("grp")
    core = column % 2
    vmem = pl.BlockSpec(memory_space=pltpu.VMEM)
    messages = pl.pallas_call(
        pack_kernel,
        out_shape=jax.ShapeDtypeStruct((columns * PER, LANES), jnp.bfloat16),
        in_specs=[vmem],
        out_specs=vmem,
        compiler_params=pltpu.CompilerParams(vmem_limit_bytes=8 * 2**20),
        cost_estimate=pl.CostEstimate(flops=2 * 10**10, bytes_accessed=3 * 2**17, transcendentals=0),
    )(records.T)
    received = lax.all_to_all(
        messages.reshape(columns, PER, LANES), "sta", split_axis=0, concat_axis=0, tiled=True
    ).reshape(columns * PER, LANES)
    band, share = band_tables()
    size = PER * ROWS
    given, other = pl.pallas_call(
        whiten_kernel,
        out_shape=(
            jax.ShapeDtypeStruct((size, LANES), jnp.bfloat16),
            jax.ShapeDtypeStruct((size, LANES), jnp.bfloat16),
        ),
        in_specs=[vmem] * 4,
        out_specs=(vmem, vmem),
        scratch_shapes=[
            pltpu.VMEM((2 * SEGMENTS * PER, POINTS), jnp.bfloat16),
            pltpu.VMEM((2 * size, LANES), jnp.float32),
        ],
        compiler_params=pltpu.CompilerParams(vmem_limit_bytes=16 * 2**20),
        cost_estimate=pl.CostEstimate(flops=2 * 10**9, bytes_accessed=3 * 2**20, transcendentals=0),
    )(received, jnp.asarray(forward_table()), jnp.asarray(band), jnp.asarray(share))
    def from_net(value, by):
        return lax.ppermute(value, "grp", [((i + by) % nets, i) for i in range(nets)])

    def from_other_core(value):
        return lax.ppermute(value, "sta", [(i, i ^ 1) for i in range(columns)])

    other3, given1 = from_net(other, 3), from_net(given, 1)
    other1, given3 = from_net(other, 1), from_net(given, 3)
    other2, given2 = from_net(other1, 1), from_net(given3, 3)
    first, third, other1 = lax.optimization_barrier((given, given3, other1))
    givens = [given, given1, given2, given3]
    pieces = givens + [other, other1, other2, other3] + [from_other_core(part) for part in (first, given1, given2, third)]

    station_net = pair_list // (columns * PER)
    offset = pair_list // PER % columns - column
    slot = jnp.where(offset == 1, 2, jnp.where(offset == 0, 1 - core, core))
    place = ((slot * nets + (station_net - net) % nets) * PER + pair_list % PER) * ROWS
    index = place.transpose(2, 0, 1).reshape(-1)
    even, odd = lag_tables()
    pairs = pair_list.shape[0] * BLOCK
    steps = pairs // STEP_PAIRS
    return pl.pallas_call(
        pair_kernel,
        out_shape=jax.ShapeDtypeStruct((pairs, POINTS), jnp.float32),
        in_specs=[pl.BlockSpec(memory_space=pltpu.SMEM)] + [vmem] * (3 + SLOTS * NETS),
        out_specs=pl.BlockSpec(memory_space=pl.ANY),
        scratch_shapes=[
            pltpu.VMEM((SLOTS * NETS * PER * ROWS, LANES), jnp.float32),
            pltpu.VMEM((STEP_PAIRS * ROWS // 4, LANES), jnp.float32),
            pltpu.VMEM((STEP_PAIRS * ROWS // 4, LANES), jnp.float32),
            pltpu.VMEM((pairs, POINTS), jnp.float32),
            pltpu.SMEM((2 * pairs,), jnp.int32),
            pltpu.SemaphoreType.DMA,
            pltpu.SemaphoreType.DMA((steps,)),
            pltpu.SemaphoreType.DMA((pairs // BLOCK,)),
        ],
        compiler_params=pltpu.CompilerParams(vmem_limit_bytes=24 * 2**20),
        cost_estimate=pl.CostEstimate(flops=6 * 10**9, bytes_accessed=6 * 2**20, transcendentals=0),
    )(live_blocks, index, jnp.asarray(even), jnp.asarray(odd), *pieces).reshape(
        pair_list.shape[0], BLOCK, POINTS
    )


def solution(mesh):
    in_specs = (P("grp", "sta"), P(("sta", "grp"), None, None), P(("sta", "grp")))
    out_specs = P(("sta", "grp"), None, None)
    return jax.shard_map(local, mesh=mesh, in_specs=in_specs, out_specs=out_specs, check_vma=False)
```

```python
import math

import jax
import jax.numpy as jnp
import ml_dtypes
import numpy as np
from jax import lax
from jax.experimental import pallas as pl
from jax.experimental.pallas import tpu as pltpu
from jax.sharding import PartitionSpec as P

SEGMENTS = 4
POINTS = 1024
BINS = 512
HALF = 16
BLOCK = 128
NETS = 4
PER = 16
SLOTS = 3
ROWS = 32
LANES = 128
STEP_PAIRS = 256
UNROLL = 64

BIN_ORDER = np.concatenate([np.arange(2, BINS + 1, 2), np.arange(1, BINS + 1, 2)])


def forward_table():
    t = np.arange(POINTS, dtype=np.int64)[:, None]
    turn = (t * BIN_ORDER[None, :] % POINTS) * (2.0 * math.pi / POINTS)
    table = np.concatenate([np.cos(turn), -np.sin(turn)], axis=1) / math.sqrt(POINTS)
    return table.astype(np.float32).astype(ml_dtypes.bfloat16)


def lag_tables():
    lag = np.arange(POINTS // 2, dtype=np.int64)[None, :] - POINTS // 2
    tables = []
    for bins in (BIN_ORDER[: BINS // 2], BIN_ORDER[BINS // 2 :]):
        turn = (bins[:, None] * lag % POINTS) * (2.0 * math.pi / POINTS)
        table = np.concatenate([np.cos(turn), -np.sin(turn)], axis=0) / math.sqrt(BINS * SEGMENTS)
        tables.append(table.astype(np.float32).astype(ml_dtypes.bfloat16))
    return tables


def band_tables():
    near = np.abs(BIN_ORDER[:, None] - BIN_ORDER[None, :]) <= HALF
    share = 1.0 / (near.sum(axis=0) * SEGMENTS)
    return near.astype(np.float32).astype(ml_dtypes.bfloat16), share.astype(np.float32)[None, :]


def pack_kernel(records_ref, out_ref):
    samples, stations = records_ref.shape
    own = records_ref[...].astype(jnp.float32)
    ahead = jnp.concatenate([own[:, 2 * PER :], own[:, : 2 * PER]], axis=1)
    both = jnp.concatenate([own, ahead], axis=0)
    for block in range(stations // LANES):
        part = both[:, block * LANES : (block + 1) * LANES]
        out_ref[block * LANES : (block + 1) * LANES, :] = part.T.astype(jnp.bfloat16)


def whiten_kernel(
    parts_ref, forward_ref, band_ref, share_ref, given_ref, other_ref, segs, wide
):
    core = lax.rem(lax.axis_index("sta"), 2)
    low = lax.broadcasted_iota(jnp.int32, (PER, LANES), 1) < LANES // 2
    for e in range(SEGMENTS):
        for u in range(POINTS // LANES):
            row = (e * POINTS // LANES + u) * 2 * PER
            first = parts_ref[row : row + PER, :].astype(jnp.float32)
            second = parts_ref[row + PER : row + 2 * PER, :].astype(jnp.float32)
            near = jnp.where(low, first, pltpu.roll(second, LANES // 2, 1))
            far = jnp.where(low, pltpu.roll(first, LANES // 2, 1), second)
            segs[e * PER : (e + 1) * PER, u * LANES : (u + 1) * LANES] = near.astype(jnp.bfloat16)
            segs[(SEGMENTS + e) * PER : (SEGMENTS + e + 1) * PER, u * LANES : (u + 1) * LANES] = (
                far.astype(jnp.bfloat16)
            )
    spectra = jnp.dot(segs[...], forward_ref[...], preferred_element_type=jnp.float32)
    squares = (spectra * spectra).reshape(2, SEGMENTS, PER, 2 * BINS)
    energy = jnp.sum(squares, axis=1).reshape(2 * PER, 2 * BINS)
    energy = energy[:, :BINS] + energy[:, BINS:]
    top = energy.astype(jnp.bfloat16)
    rest = energy - top.astype(jnp.float32)
    middle = rest.astype(jnp.bfloat16)
    bottom = (rest - middle.astype(jnp.float32)).astype(jnp.bfloat16)
    split = jnp.concatenate([top, middle, bottom], axis=0)
    sums = jnp.dot(split, band_ref[...], preferred_element_type=jnp.float32)
    count = 2 * PER
    total = sums[:count] + (sums[count : 2 * count] + sums[2 * count :])
    scale = lax.rsqrt(total * share_ref[...] + 1e-06)
    for column in range(2):
        for e in range(SEGMENTS):
            for k in range(0, PER, 8):
                for part in range(2):
                    for j in range(BINS // LANES):
                        at = (column * SEGMENTS + e) * PER + k
                        lane = part * BINS + j * LANES
                        piece = (
                            spectra[at : at + 8, lane : lane + LANES]
                            * scale[column * PER + k : column * PER + k + 8, j * LANES : (j + 1) * LANES]
                        )
                        row = (column * PER + k) * ROWS + part * (ROWS // 2) + e * (BINS // LANES) + j
                        wide[pl.ds(row, 8, stride=ROWS), :] = piece
    size = PER * ROWS
    given = 1 - core
    given_ref[...] = wide[pl.ds(pl.multiple_of(given * size, size), size), :].astype(jnp.bfloat16)
    other_ref[...] = wide[pl.ds(pl.multiple_of(core * size, size), size), :].astype(jnp.bfloat16)


def pair_kernel(live_ref, index_ref, even_ref, odd_ref, *refs):
    sources, (out_ref, *scratch) = refs[: SLOTS * NETS], refs[SLOTS * NETS :]
    table, reals, imags, result, places, place_sem, sems, block_sems = scratch
    size = PER * ROWS
    half = ROWS // 4
    pairs = index_ref.shape[0] // 2
    load_places = pltpu.make_async_copy(index_ref, places, place_sem)
    load_places.start()
    live = jnp.minimum(live_ref[0], pairs // BLOCK)
    full = lax.div(live, STEP_PAIRS // BLOCK)

    def send(step, count, which):
        rows = pl.ds(pl.multiple_of(step * count, count), count)
        return pltpu.make_async_copy(result.at[rows], out_ref.at[rows], which.at[step])

    def clear(block, carry):
        rows = pl.ds(pl.multiple_of(block * BLOCK, BLOCK), BLOCK)
        result[rows, :] = jnp.zeros((BLOCK, POINTS), jnp.float32)
        send(block, BLOCK, block_sems).start()
        return carry

    lax.fori_loop(live, pairs // BLOCK, clear, 0)
    for n, source in enumerate(sources):
        table[n * size : (n + 1) * size, :] = source[...].astype(jnp.float32)
    load_places.wait()

    def mix(first_pair, q):
        at = first_pair + q
        first = table[pl.ds(pl.multiple_of(places[at], ROWS), ROWS), :]
        second = table[pl.ds(pl.multiple_of(places[pairs + at], ROWS), ROWS), :]
        ar0, ar1, ai0, ai1 = (first[n : n + half] for n in range(0, ROWS, half))
        br0, br1, bi0, bi1 = (second[n : n + half] for n in range(0, ROWS, half))
        rows = pl.ds(pl.multiple_of(q * half, half), half)
        reals[rows, :] = (ar0 * br0 + ar1 * br1) + (ai0 * bi0 + ai1 * bi1)
        imags[rows, :] = (ai0 * br0 + ai1 * br1) - (ar0 * bi0 + ar1 * bi1)

    def rows_of(first_block, count):
        blocks = []
        for part in (reals, imags):
            for b in (first_block, first_block + 1):
                low = part[pl.ds(b, count, stride=half), :]
                high = part[pl.ds(b + half // 2, count, stride=half), :]
                blocks.append((low + high).astype(jnp.bfloat16))
        return jnp.concatenate(blocks, axis=1)

    def work(step, count, which):
        def some(g, inner):
            for q in range(UNROLL):
                mix(step * count, g * UNROLL + q)
            return inner

        lax.fori_loop(0, count // UNROLL, some, 0)
        even = jnp.dot(rows_of(0, count), even_ref[...], preferred_element_type=jnp.float32)
        odd = jnp.dot(rows_of(2, count), odd_ref[...], preferred_element_type=jnp.float32)
        here = pl.ds(pl.multiple_of(step * count, count), count)
        result[here, : POINTS // 2] = even + odd
        result[here, POINTS // 2 :] = even - odd
        send(step, count, which).start()

    def run(step, carry):
        work(step, STEP_PAIRS, sems)
        return carry

    def finish(step, carry):
        send(step, STEP_PAIRS, sems).wait()
        return carry

    def finish_block(block, carry):
        send(block, BLOCK, block_sems).wait()
        return carry

    lax.fori_loop(0, full, run, 0)

    @pl.when(full * (STEP_PAIRS // BLOCK) < live)
    def _():
        work(live - 1, BLOCK, block_sems)

    lax.fori_loop(0, full, finish, 0)
    lax.fori_loop(full * (STEP_PAIRS // BLOCK), pairs // BLOCK, finish_block, 0)


def local(records, pair_list, live_blocks):
    columns = lax.axis_size("sta")
    nets = lax.axis_size("grp")
    column = lax.axis_index("sta")
    net = lax.axis_index("grp")
    core = column % 2
    vmem = pl.BlockSpec(memory_space=pltpu.VMEM)
    messages = pl.pallas_call(
        pack_kernel,
        out_shape=jax.ShapeDtypeStruct((columns * PER, LANES), jnp.bfloat16),
        in_specs=[vmem],
        out_specs=vmem,
        compiler_params=pltpu.CompilerParams(vmem_limit_bytes=8 * 2**20),
        cost_estimate=pl.CostEstimate(flops=2 * 10**10, bytes_accessed=3 * 2**17, transcendentals=0),
    )(records.T)
    received = lax.all_to_all(
        messages.reshape(columns, PER, LANES), "sta", split_axis=0, concat_axis=0, tiled=True
    ).reshape(columns * PER, LANES)
    band, share = band_tables()
    size = PER * ROWS
    given, other = pl.pallas_call(
        whiten_kernel,
        out_shape=(
            jax.ShapeDtypeStruct((size, LANES), jnp.bfloat16),
            jax.ShapeDtypeStruct((size, LANES), jnp.bfloat16),
        ),
        in_specs=[vmem] * 4,
        out_specs=(vmem, vmem),
        scratch_shapes=[
            pltpu.VMEM((2 * SEGMENTS * PER, POINTS), jnp.bfloat16),
            pltpu.VMEM((2 * size, LANES), jnp.float32),
        ],
        compiler_params=pltpu.CompilerParams(vmem_limit_bytes=16 * 2**20),
        cost_estimate=pl.CostEstimate(flops=2 * 10**9, bytes_accessed=3 * 2**20, transcendentals=0),
    )(received, jnp.asarray(forward_table()), jnp.asarray(band), jnp.asarray(share))
    def from_net(value, by):
        return lax.ppermute(value, "grp", [((i + by) % nets, i) for i in range(nets)])

    def from_other_core(value):
        return lax.ppermute(value, "sta", [(i, i ^ 1) for i in range(columns)])

    other3, given1 = from_net(other, 3), from_net(given, 1)
    other1, given3 = from_net(other, 1), from_net(given, 3)
    other2, given2 = from_net(other1, 1), from_net(given3, 3)
    first, third, other1 = lax.optimization_barrier((given, given3, other1))
    swap3, swap0, swap1 = (from_other_core(part) for part in (third, first, given1))
    swaps = [swap0, swap1, from_other_core(given2), swap3]
    pieces = [given, given1, given2, given3, other, other1, other2, other3] + swaps

    station_net = pair_list // (columns * PER)
    offset = pair_list // PER % columns - column
    slot = jnp.where(offset == 1, 2, jnp.where(offset == 0, 1 - core, core))
    place = ((slot * nets + (station_net - net) % nets) * PER + pair_list % PER) * ROWS
    index = place.transpose(2, 0, 1).reshape(-1)
    even, odd = lag_tables()
    pairs = pair_list.shape[0] * BLOCK
    steps = pairs // STEP_PAIRS
    return pl.pallas_call(
        pair_kernel,
        out_shape=jax.ShapeDtypeStruct((pairs, POINTS), jnp.float32),
        in_specs=[pl.BlockSpec(memory_space=pltpu.SMEM)] + [vmem] * (3 + SLOTS * NETS),
        out_specs=pl.BlockSpec(memory_space=pl.ANY),
        scratch_shapes=[
            pltpu.VMEM((SLOTS * NETS * PER * ROWS, LANES), jnp.float32),
            pltpu.VMEM((STEP_PAIRS * ROWS // 4, LANES), jnp.float32),
            pltpu.VMEM((STEP_PAIRS * ROWS // 4, LANES), jnp.float32),
            pltpu.VMEM((pairs, POINTS), jnp.float32),
            pltpu.SMEM((2 * pairs,), jnp.int32),
            pltpu.SemaphoreType.DMA,
            pltpu.SemaphoreType.DMA((steps,)),
            pltpu.SemaphoreType.DMA((pairs // BLOCK,)),
        ],
        compiler_params=pltpu.CompilerParams(vmem_limit_bytes=24 * 2**20),
        cost_estimate=pl.CostEstimate(flops=6 * 10**9, bytes_accessed=6 * 2**20, transcendentals=0),
    )(live_blocks, index, jnp.asarray(even), jnp.asarray(odd), *pieces).reshape(
        pair_list.shape[0], BLOCK, POINTS
    )


def solution(mesh):
    in_specs = (P("grp", "sta"), P(("sta", "grp"), None, None), P(("sta", "grp")))
    out_specs = P(("sta", "grp"), None, None)
    return jax.shard_map(local, mesh=mesh, in_specs=in_specs, out_specs=out_specs, check_vma=False)
```
